128 devices in a mesh: ta: 4 (over y), gx: 8 (over z, core), gy: 4 (over x).
Axes of the slice: x: 4, y: 4, z: 4, core: 2. Of those that a mesh axis runs over, the one named last changes fastest.
Arguments:
- feat: bfloat16 [4, 8, 4, 768, 128], P('ta', 'gx', 'gy'), may hold values from -6 to 6
- ref_feat: bfloat16 [4, 8, 4, 768, 128], P('ta', 'gx', 'gy'), may hold values from -6 to 6
- rim_rows: int32 [4, 8, 4, 48], P('ta', 'gx', 'gy'), may hold values from 0 to 767
- nbr: int32 [4, 8, 4, 27, 768], P('ta', 'gx', 'gy'), may hold values from 0 to 1200, as said below
- send_blocks: int32 [4, 8, 4, 32, 2], P('ta', 'gx', 'gy'), may hold values from 0 to 5
- send_count: int32 [4, 8, 4, 32], P('ta', 'gx', 'gy'), may hold values from 0 to 2, as said below
- match_slot: int32 [4, 8, 4, 6], P('ta', 'gx', 'gy'), may hold values from 0 to 64, as said below
- labels: int32 [4, 8, 4, 768], P('ta', 'gx', 'gy'), may hold values 0 or 1
- conv_weight: bfloat16 [27, 128, 128], replicated, may hold values from -0.109375 to 0.109375
- ref_weight: bfloat16 [128, 128], replicated, may hold values from -0.5 to 0.5
- cls_weight: bfloat16 [128], replicated, may hold values from -1.796875 to 1.796875
Outputs:
- features_out: bfloat16 [4, 8, 4, 768, 128], P('ta', 'gx', 'gy')
- feature_grad: bfloat16 [4, 8, 4, 768, 128], P('ta', 'gx', 'gy')
- weight_grad: float32 [27, 128, 128], replicated
- ref_grad: float32 [128, 128], replicated
The draws below stay inside these ranges and needn't reach their ends.
Inputs may be any that keep to these rules, and one draw needn't show every extreme that they name: `nbr`: rows index the brick's 768 rows, then the 432 rim rows of the 3 x 3 bricks around it (x outer, own brick in the middle), then the zero row; offset 13 of a voxel is the voxel itself. `send_count`: every brick sends 2 blocks to its own brick, and in each frame one brick drawn from the seed receives 2 blocks from every brick. `match_slot`: 64 means no match; every brick has one or more unmatched blocks.
All inputs are finite; a program needn't handle non-finite values. No bound on the sum of `labels` on one device may be relied on, other than what follows from the above.
Results may differ from the reference program's by a relative error of at most 0.0053.
Values may be sent and summed in bfloat16 or wider, within the bound.
No kernel may reach another device: no remote copies, remote signals or barrier semaphores. Data moves between devices by JAX's collectives and lax.ppermute only.
A program may use at most 64 MiB of HBM per device.

```python
import jax
import jax.numpy as jnp
from jax import lax

CHANNELS = 128
OFFSETS = 27
BLOCK = 128
CAP = 2
NB = 6
ROWS = 768
HALO = 48
FRAMES = 4
XBRICKS = 8
YBRICKS = 4
DESTS = 32


def draw_nbr(key, part):
    key_kind, key_local, key_halo = jax.random.split(jax.random.fold_in(key, 11), 3)
    dims = (FRAMES, XBRICKS, YBRICKS, OFFSETS, ROWS)
    choose = jax.random.randint(key_kind, dims, 0, 8)
    local = jax.random.randint(key_local, dims, 0, ROWS)
    remote = ROWS + jax.random.randint(key_halo, dims, 0, 9 * HALO)
    picked = jnp.where(choose == 0, ROWS + 9 * HALO, jnp.where(choose <= 2, remote, local))
    itself = jnp.broadcast_to(jnp.arange(ROWS, dtype=jnp.int32).reshape(1, 1, 1, 1, ROWS), dims)
    offset = jnp.arange(OFFSETS, dtype=jnp.int32).reshape(1, 1, 1, OFFSETS, 1)
    return jnp.where(offset == 13, itself, picked).astype(jnp.int32)


def draw_send_count(key, part):
    key_count, key_hot = jax.random.split(jax.random.fold_in(key, 23))
    counts = jax.random.randint(key_count, (FRAMES, XBRICKS, YBRICKS, DESTS), 0, CAP + 1)
    hottest = jax.random.randint(key_hot, (FRAMES, 1, 1, 1), 0, DESTS)
    own_brick = (jnp.arange(XBRICKS)[:, None] * YBRICKS + jnp.arange(YBRICKS)[None, :])[None, :, :, None]
    target = jnp.arange(DESTS).reshape(1, 1, 1, DESTS)
    return jnp.where((target == own_brick) | (target == hottest), CAP, counts).astype(jnp.int32)


def draw_match_slot(key, part):
    key_slot, key_empty = jax.random.split(jax.random.fold_in(key, 37))
    slots = jax.random.randint(key_slot, (FRAMES, XBRICKS, YBRICKS, NB), 0, DESTS * CAP + 1)
    empty = jax.random.randint(key_empty, (FRAMES, XBRICKS, YBRICKS, 1), 0, NB)
    blocks = jnp.arange(NB).reshape(1, 1, 1, NB)
    return jnp.where(blocks == empty, DESTS * CAP, slots).astype(jnp.int32)


def plant(result, key, low, high):
    shape = result.shape
    place = [jax.random.randint(jax.random.fold_in(key, axis), (), 0, shape[axis]) for axis in range(len(shape))]
    result = result.at[tuple(place)].set(low)
    longest = shape.index(max(shape))
    place[longest] = (place[longest] + 1) % shape[longest]
    return result.at[tuple(place)].set(high)


def level_of(stream_key, extent, cuts, low, top_value):
    gain = 1.0
    for position, shards_of in cuts:
        steps = jax.random.uniform(jax.random.fold_in(jax.random.fold_in(stream_key, 6), position), (shards_of,), jnp.float32, low / len(cuts), top_value / len(cuts))
        gain = gain * jnp.repeat(jnp.exp(steps), extent[position] // shards_of).reshape((-1,) + (1,) * (len(extent) - 1 - position))
    return gain


def noise(own_key, shape, spread, limit, cuts=(), kind=jnp.bfloat16):
    array = spread * jax.random.normal(own_key, shape, jnp.float32)
    if cuts:
        array = array * level_of(own_key, shape, cuts, -0.22, 0.18)
    return jnp.clip(array, -limit, limit).astype(kind)


def setup_inputs(seed: int = 0) -> dict:
    seeds = jax.random.split(jax.random.key(seed), 12)
    return {
        "feat": noise(seeds[0], (FRAMES, XBRICKS, YBRICKS, ROWS, CHANNELS), 1.0, 6.0, ((0, 4), (1, 8), (2, 4))),
        "ref_feat": noise(seeds[1], (FRAMES, XBRICKS, YBRICKS, ROWS, CHANNELS), 1.0, 6.0, ((0, 4), (1, 8), (2, 4))),
        "rim_rows": plant(jax.random.randint(seeds[2], (FRAMES, XBRICKS, YBRICKS, HALO), 0, ROWS), jax.random.fold_in(seeds[2], 1), 0, ROWS - 1).astype(jnp.int32),
        "nbr": draw_nbr(jax.random.fold_in(seeds[11], 71), 0),
        "send_blocks": plant(jax.random.randint(seeds[4], (FRAMES, XBRICKS, YBRICKS, DESTS, CAP), 0, NB), jax.random.fold_in(seeds[4], 1), 0, NB - 1).astype(jnp.int32),
        "send_count": draw_send_count(jax.random.fold_in(seeds[11], 71), 0),
        "match_slot": draw_match_slot(jax.random.fold_in(seeds[11], 71), 0),
        "labels": plant((jax.random.randint(seeds[7], (FRAMES, XBRICKS, YBRICKS, ROWS), 0, 2) < 1).astype(jnp.int32), jax.random.fold_in(seeds[7], 1), 0, 1),
        "conv_weight": noise(seeds[8], (OFFSETS, CHANNELS, CHANNELS), (OFFSETS * CHANNELS) ** -0.5, 0.109375),
        "ref_weight": noise(seeds[9], (CHANNELS, CHANNELS), CHANNELS ** -0.5, 0.5),
        "cls_weight": noise(seeds[10], (CHANNELS,), 0.3, 1.796875),
    }


loss_scale = 16.0


def pick_rows(source, index):
    return source[index]


def add_rows(target, index, values):
    return target.at[index].add(values)


def brick_pass(current, halo_block, matched, offsets_map, label_row, conv_weight, ref_weight, cls_weight):
    channels = current.shape[1]
    extended = jnp.concatenate([current, halo_block.reshape(-1, channels), jnp.zeros((1, channels), current.dtype)], axis=0)

    def forward_step(total, pair):
        index_row, weight = pair
        return total + jnp.dot(extended[index_row], weight, preferred_element_type=jnp.float32), None

    conv_sum = lax.scan(forward_step, jnp.zeros((current.shape[0], channels), jnp.float32), (offsets_map, conv_weight))[0]
    preact = conv_sum + jnp.dot(matched, ref_weight, preferred_element_type=jnp.float32)
    activ = jax.nn.silu(preact).astype(jnp.bfloat16)
    logits = jnp.dot(activ, cls_weight, preferred_element_type=jnp.float32)
    resid = jax.nn.sigmoid(logits) - label_row.astype(jnp.float32)
    sigmas = jax.nn.sigmoid(preact)
    pre_grad = (loss_scale * resid[:, None] * cls_weight.astype(jnp.float32)[None, :] * sigmas * (1.0 + preact * (1.0 - sigmas))).astype(jnp.bfloat16)

    def backward_step(grads, pair):
        index_row, weight = pair
        gathered = extended[index_row]
        weight_term = jnp.dot(gathered.T, pre_grad, preferred_element_type=jnp.float32)
        input_term = jnp.dot(pre_grad, weight.T, preferred_element_type=jnp.float32)
        return grads.at[index_row].add(input_term), weight_term

    ext_grad, weight_terms = lax.scan(backward_step, jnp.zeros((extended.shape[0], channels), jnp.float32), (offsets_map, conv_weight))
    ref_term = jnp.dot(matched.T, pre_grad, preferred_element_type=jnp.float32)
    rows_here = current.shape[0]
    return activ, ext_grad[:rows_here], ext_grad[rows_here:rows_here + halo_block.shape[0] * halo_block.shape[1]], weight_terms, ref_term


def reference(feat, ref_feat, rim_rows, nbr, send_blocks, send_count, match_slot, labels, conv_weight, ref_weight, cls_weight):
    devices_all = FRAMES * XBRICKS * YBRICKS
    rims = jax.vmap(pick_rows)(feat.reshape(devices_all, ROWS, CHANNELS), rim_rows.reshape(devices_all, HALO))
    rims = rims.reshape(FRAMES, XBRICKS, YBRICKS, HALO, CHANNELS)
    padded = jnp.pad(rims, ((0, 0), (1, 1), (1, 1), (0, 0), (0, 0)))
    halos = jnp.stack([padded[:, slot_x:slot_x + XBRICKS, slot_y:slot_y + YBRICKS] for slot_x in range(3) for slot_y in range(3)], axis=3)
    halos = halos.reshape(devices_all, 9, HALO, CHANNELS)

    blocks = ref_feat.reshape(devices_all, NB, BLOCK, CHANNELS)
    lists = send_blocks.reshape(devices_all, DESTS * CAP)
    picked = jax.vmap(pick_rows)(blocks, lists)
    keep = jnp.arange(CAP)[None, None, :] < send_count.reshape(devices_all, DESTS)[:, :, None]
    keep = keep.reshape(devices_all, DESTS * CAP)[:, :, None, None]
    picked = jnp.where(keep, picked, jnp.zeros_like(picked))
    picked = picked.reshape(FRAMES, DESTS, DESTS, CAP, BLOCK, CHANNELS).transpose(0, 2, 1, 3, 4, 5)
    received = jnp.concatenate([jnp.zeros_like(picked[:1]), picked[:-1]], axis=0)
    received = received.reshape(devices_all, DESTS * CAP, BLOCK, CHANNELS)
    table = jnp.concatenate([received, jnp.zeros((devices_all, 1, BLOCK, CHANNELS), received.dtype)], axis=1)
    matched = jax.vmap(pick_rows)(table, match_slot.reshape(devices_all, NB)).reshape(devices_all, ROWS, CHANNELS)

    def per_device(totals, inputs):
        current, halo_block, matched_rows, offsets_map, label_row = inputs
        activ, local_grad, halo_grad, weight_terms, ref_term = brick_pass(current, halo_block, matched_rows, offsets_map, label_row, conv_weight, ref_weight, cls_weight)
        return (totals[0] + weight_terms, totals[1] + ref_term), (activ, local_grad, halo_grad)

    start = (jnp.zeros((OFFSETS, CHANNELS, CHANNELS), jnp.float32), jnp.zeros((CHANNELS, CHANNELS), jnp.float32))
    inputs = (feat.reshape(devices_all, ROWS, CHANNELS), halos, matched, nbr.reshape(devices_all, OFFSETS, ROWS), labels.reshape(devices_all, ROWS))
    totals, outputs = lax.scan(per_device, start, inputs)
    activ, local_grad, halo_grad = outputs
    halo_grad = halo_grad.reshape(FRAMES, XBRICKS, YBRICKS, 3, 3, HALO, CHANNELS)
    halo_pad = jnp.pad(halo_grad, ((0, 0), (1, 1), (1, 1), (0, 0), (0, 0), (0, 0), (0, 0)))
    rim_grad = jnp.zeros((FRAMES, XBRICKS, YBRICKS, HALO, CHANNELS), jnp.float32)
    for slot_x in range(3):
        for slot_y in range(3):
            rim_grad = rim_grad + halo_pad[:, 2 - slot_x:2 - slot_x + XBRICKS, 2 - slot_y:2 - slot_y + YBRICKS, slot_x, slot_y]
    feature_grad = jax.vmap(add_rows)(local_grad, rim_rows.reshape(devices_all, HALO), rim_grad.reshape(devices_all, HALO, CHANNELS))
    shape_out = (FRAMES, XBRICKS, YBRICKS, ROWS, CHANNELS)
    return activ.reshape(shape_out), feature_grad.astype(jnp.bfloat16).reshape(shape_out), totals[0], totals[1]
```

```python
import jax
import jax.numpy as jnp
from jax import lax
from jax.experimental import pallas as pl
from jax.experimental.pallas import tpu as pltpu
from jax.sharding import Mesh
from jax.sharding import PartitionSpec as P

BF = jnp.bfloat16
F32 = jnp.float32
I16 = jnp.int16
BLOCK = 128
LANES = 128
CAP = 2
GROUP = 9
LOSS_SCALE = 16.0
VM = pl.BlockSpec(memory_space=pltpu.VMEM)
SM = pl.BlockSpec(memory_space=pltpu.SMEM)
NT = (((1,), (1,)), ((), ()))
TN = (((0,), (0,)), ((), ()))
X = ("gz", "gc")
PLANE = ("gz", "gc", "gy")
REST = ("ta", "gz", "gy")


def params():
    return pltpu.CompilerParams(vmem_limit_bytes=48 * 1024 * 1024)


def cost(flops, moved):
    return pl.CostEstimate(flops=int(flops), bytes_accessed=int(moved), transcendentals=0)


def iota(shape, dim):
    return lax.broadcasted_iota(jnp.int32, shape, dim)


def dot(left, right):
    return jnp.dot(left, right, preferred_element_type=F32)


def hot_of(mask):
    return jnp.where(mask, jnp.ones((), BF), jnp.zeros((), BF))


def lane_hot(column, width):
    n = column.shape[0]
    lane = iota((n, LANES), 1)
    pieces = []
    for start in range(0, width, LANES):
        piece = hot_of(column - start == lane)
        pieces.append(piece[:, : min(LANES, width - start)])
    return jnp.concatenate(pieces, axis=1) if len(pieces) > 1 else pieces[0]


def sublane_hot(row16, start, height, width):
    base = iota((height, width), 0).astype(I16)
    rows = row16 - jnp.asarray(start, I16)
    wide = jnp.broadcast_to(rows[None], (height // 16, 16, width)).reshape(height, width)
    return hot_of(wide == base)


def pack_kernel(shift_ref, match_ref, rim_ref, current_ref, out_ref):
    bricks = out_ref.shape[0]
    step = BLOCK // bricks
    n = bricks * 32
    rows = iota((n, LANES), 0)
    i, j = rows // 32, rows % 32
    blocks = current_ref.shape[0] // BLOCK
    used = blocks * step
    target = jnp.where(
        j < used,
        (j // step) * BLOCK + i * step + j % step,
        jnp.where(j == used, blocks * BLOCK, -1),
    )
    hot = lane_hot(target, shift_ref.shape[0])
    out = dot(hot, shift_ref[...])
    out = jnp.where(j == used + 1, match_ref[...], out).astype(BF)
    out_ref[:, 0:32, :] = out.reshape(bricks, 32, LANES)
    count = rim_ref.shape[0]
    rim_column = jnp.broadcast_to(rim_ref[...], (count, LANES))
    rim = dot(lane_hot(rim_column, current_ref.shape[0]), current_ref[...]).astype(BF)
    for brick in range(bricks):
        out_ref[brick, 32 : 32 + count, :] = rim


def select_kernel(blocks, recv_ref, out_ref):
    bricks = out_ref.shape[0]
    step = BLOCK // bricks
    used = blocks * step
    n = bricks * 32
    tail = recv_ref[:, 16:32, :].astype(F32)
    which = iota(tail.shape, 1)
    coded = jnp.sum(jnp.where(which == used - 16, tail, 0.0), axis=1).astype(BF)
    slots = jnp.sum(jnp.where(which == used - 15, tail, 0.0), axis=1).astype(BF)
    rows = iota((n, LANES), 0)
    lane = iota((n, LANES), 1)
    d, j = rows // 32, rows % 32
    own = hot_of(d == lane)[:, :bricks]
    listed = dot(own, slots)
    slot = jnp.sum(jnp.where(lane == j // step, listed, 0.0), axis=1, keepdims=True)
    slot = jnp.broadcast_to(slot, (n, LANES)).astype(jnp.int32)
    entry = hot_of(lane == d * CAP + slot % CAP)
    codes = lax.dot_general(entry, coded, NT, preferred_element_type=F32)
    source = slot // CAP
    code = jnp.sum(
        jnp.where(lane[:, :bricks] == source[:, :bricks], codes, 0.0), axis=1, keepdims=True
    )
    code = jnp.broadcast_to(code, (n, LANES)).astype(jnp.int32)
    live = (slot < bricks * CAP) & (code < blocks) & (j < used)
    index = jnp.where(live, source * 32 + code * step + j % step, -1)
    data = recv_ref[:, 0:32, :].reshape(n, LANES)
    out_ref[...] = dot(lane_hot(index, n), data).astype(BF).reshape(out_ref.shape)


def local_kernel(idx_ref, current_ref, out_ref, turned_ref):
    @pl.when(pl.program_id(0) == 0)
    def _():
        turned_ref[...] = current_ref[...].T

    height, width = current_ref.shape[0], out_ref.shape[1]
    for o in range(GROUP):
        hot = sublane_hot(idx_ref[o], 0, height, width)
        out_ref[o * LANES : (o + 1) * LANES, :] = dot(turned_ref[...], hot).astype(BF)


def halo_kernel(
    xcount, ycount, place_ref, idx_ref, recv_ref, local_ref, w_ref, out_ref, conv_ref, turned_ref
):
    width = out_ref.shape[1]
    rim = recv_ref.shape[1] - 32

    @pl.when(pl.program_id(0) == 0)
    def _():
        conv_ref[...] = jnp.zeros_like(conv_ref)
        pieces = []
        for i in range(3):
            for j in range(3):
                a = place_ref[0] + (i - 1)
                b = place_ref[1] + (j - 1)
                inside = (a >= 0) & (a < xcount) & (b >= 0) & (b < ycount)
                q = jnp.clip(a, 0, xcount - 1) * ycount + jnp.clip(b, 0, ycount - 1)
                piece = recv_ref[q, 32 : 32 + rim, :].astype(F32)
                pieces.append(jnp.where(inside, piece, 0.0))
        turned_ref[...] = jnp.concatenate(pieces, axis=0).astype(BF).T

    for o in range(GROUP):
        hot = sublane_hot(idx_ref[o], width, 9 * rim, width)
        part = dot(turned_ref[...], hot).astype(BF)
        span = slice(o * LANES, (o + 1) * LANES)
        out_ref[span, :] = local_ref[span, :] + part
    conv_ref[...] += lax.dot_general(w_ref[...], out_ref[...], TN, preferred_element_type=F32)


def point_kernel(
    core_ref, conv_ref, recv_ref, label_ref, ref_w_ref, cls_ref, gathered_ref,
    activ_ref, grad_ref, mine_ref, other_ref,
):
    width = conv_ref.shape[1]
    core = core_ref[0]
    half = mine_ref.shape[0]
    step_id = pl.program_id(0)
    per_step = gathered_ref.shape[0]

    def put(first, value):
        into_mine = (first // half) == core
        at = pl.ds(pl.multiple_of(first % half, LANES), value.shape[0])

        @pl.when(into_mine)
        def _():
            mine_ref[at, :] = value

        @pl.when(jnp.logical_not(into_mine))
        def _():
            other_ref[at, :] = value

    @pl.when(step_id == 0)
    def _():
        mine_ref[...] = jnp.zeros_like(mine_ref)
        other_ref[...] = jnp.zeros_like(other_ref)
        bricks = recv_ref.shape[0] // 32
        step = BLOCK // bricks
        v = iota((recv_ref.shape[0], width), 1)
        s = iota((recv_ref.shape[0], width), 0)
        place = ((v % BLOCK) // step) * 32 + (v // BLOCK) * step + v % step
        matched = dot(recv_ref[...].T, hot_of(place == s)).astype(BF)
        preact = conv_ref[...] + lax.dot_general(
            ref_w_ref[...], matched, TN, preferred_element_type=F32
        )
        cls = cls_ref[...]
        sig = jax.nn.sigmoid(preact)
        activ = (preact * sig).astype(BF)
        wide = activ.astype(F32)
        logits = jnp.sum(wide * cls, axis=0, keepdims=True)
        resid = jax.nn.sigmoid(logits) - label_ref[...].astype(F32)
        grad = LOSS_SCALE * resid * cls * sig * (1.0 + preact * (1.0 - sig))
        activ_ref[...] = wide.T.astype(BF)
        grad_ref[...] = grad.T.astype(BF)
        put(per_step * pl.num_programs(0), dot(matched, grad_ref[...]).astype(BF))

    terms = dot(gathered_ref[...], grad_ref[...]).astype(BF)
    for o in range(per_step // LANES):
        put(step_id * per_step + o * LANES, terms[o * LANES : (o + 1) * LANES])


def rim_grad_kernel(start, idx_ref, grad_ref, w_ref, spread_ref, low_ref, mid_ref, high_ref, acc_ref):
    width = grad_ref.shape[0]
    step_id = pl.program_id(0)

    @pl.when(step_id == 0)
    def _():
        acc_ref[...] = jnp.zeros_like(acc_ref)

    for o in range(GROUP):
        weight = w_ref[o * LANES : (o + 1) * LANES, :]
        part = lax.dot_general(grad_ref[...], weight, NT, preferred_element_type=F32)
        spread_ref[o * width : (o + 1) * width, :] = part.astype(BF)
    height = acc_ref.shape[0]
    hot = jnp.concatenate(
        [sublane_hot(idx_ref[o], start, height, width) for o in range(GROUP)], axis=1
    )
    acc_ref[...] += dot(hot, spread_ref[...])

    @pl.when(step_id == pl.num_programs(0) - 1)
    def _():
        third = height // 3
        low_ref[...] = acc_ref[0:third, :].astype(BF)
        mid_ref[...] = acc_ref[third : 2 * third, :]
        high_ref[...] = acc_ref[2 * third : 3 * third, :].astype(BF)


def own_grad_kernel(idx_ref, spread_ref, out_ref):
    @pl.when(pl.program_id(0) == 0)
    def _():
        out_ref[...] = jnp.zeros_like(out_ref)

    height, width = out_ref.shape[0], idx_ref.shape[2]
    piece = 256
    for start in range(0, height, piece):
        hot = jnp.concatenate(
            [sublane_hot(idx_ref[o], start, piece, width) for o in range(GROUP)], axis=1
        )
        out_ref[start : start + piece, :] += dot(hot, spread_ref[...])


def join_kernel(own_ref, mid_ref, low_ref, high_ref, rim_ref, out_ref):
    total = mid_ref[...] + low_ref[...].astype(F32) + high_ref[...].astype(F32)
    upper = total.astype(BF)
    lower = (total - upper.astype(F32)).astype(BF)
    height, count = own_ref.shape[0], total.shape[0]
    hot = hot_of(iota((height, LANES), 0) == rim_ref[...])[:, :count]
    out_ref[...] = (own_ref[...] + dot(hot, upper) + dot(hot, lower)).astype(BF)


def shifted(block, axis, count, distance):
    route = [(i - distance, i) for i in range(count) if 0 <= i - distance < count]
    return lax.ppermute(block, axis, route)


def per_device(
    feat,
    ref_feat,
    rim_rows,
    nbr,
    send_blocks,
    send_count,
    match_slot,
    labels,
    conv_weight,
    ref_weight,
    cls_weight,
):
    current = feat[0, 0, 0]
    rows, channels = current.shape
    blocks = rows // BLOCK
    rim_index = rim_rows[0, 0, 0]
    rim = rim_index.shape[0]
    offsets = nbr.shape[3]
    frames, ycount = lax.axis_size("ta"), lax.axis_size("gy")
    xcount = lax.axis_size(X)
    bricks = xcount * ycount
    halo = 9 * rim

    live = jnp.arange(CAP, dtype=jnp.int32)[None, :] < send_count[0, 0, 0][:, None]
    coded = jnp.where(live, send_blocks[0, 0, 0], blocks).reshape(1, bricks * CAP)
    coded = jnp.pad(coded.astype(BF), ((0, 15), (0, channels - bricks * CAP)))
    source = jnp.concatenate([ref_feat[0, 0, 0], coded], axis=0)
    source = shifted(source, "ta", frames, 1)
    slots = jnp.pad(match_slot[0, 0, 0].astype(F32)[None, :], ((0, 0), (0, channels - blocks)))
    packed = pl.pallas_call(
        pack_kernel,
        out_shape=jax.ShapeDtypeStruct((bricks, 32 + rim, channels), BF),
        in_specs=[VM] * 4,
        out_specs=VM,
        compiler_params=params(),
    )(source, slots, rim_index[:, None], current)
    first = lax.all_to_all(packed, PLANE, split_axis=0, concat_axis=0, tiled=True)

    index16 = jnp.broadcast_to(nbr[0, 0, 0].astype(I16)[:, None, :], (offsets, 16, rows))
    groups = offsets // GROUP
    stack = conv_weight.reshape(offsets * channels, channels)
    index_spec = pl.BlockSpec((GROUP, 16, rows), lambda g: (g, 0, 0))
    gather_spec = pl.BlockSpec((GROUP * channels, rows), lambda g: (g, 0))
    weight_spec = pl.BlockSpec((GROUP * channels, channels), lambda g: (g, 0))

    def whole(*shape):
        return pl.BlockSpec(shape, lambda g: (0,) * len(shape))

    local = pl.pallas_call(
        local_kernel,
        grid=(groups,),
        out_shape=jax.ShapeDtypeStruct((offsets * channels, rows), BF),
        in_specs=[index_spec, whole(rows, channels)],
        out_specs=gather_spec,
        scratch_shapes=[pltpu.VMEM((channels, rows), BF)],
        compiler_params=params(),
        cost_estimate=cost(4 * offsets * rows * rows * channels, 6e6),
    )(index16, current)

    chosen = pl.pallas_call(
        lambda recv_ref, out_ref: select_kernel(blocks, recv_ref, out_ref),
        out_shape=jax.ShapeDtypeStruct((bricks, 32, channels), BF),
        in_specs=[VM],
        out_specs=VM,
        compiler_params=params(),
    )(first)
    second = lax.all_to_all(chosen, PLANE, split_axis=0, concat_axis=0, tiled=True)

    place = jnp.stack([lax.axis_index(X), lax.axis_index("gy")]).astype(jnp.int32)
    gathered, conv = pl.pallas_call(
        lambda *refs: halo_kernel(xcount, ycount, *refs),
        grid=(groups,),
        out_shape=(
            jax.ShapeDtypeStruct((offsets * channels, rows), BF),
            jax.ShapeDtypeStruct((channels, rows), F32),
        ),
        in_specs=[
            SM,
            index_spec,
            whole(bricks, 32 + rim, channels),
            gather_spec,
            weight_spec,
        ],
        out_specs=(gather_spec, whole(channels, rows)),
        scratch_shapes=[pltpu.VMEM((channels, halo), BF)],
        compiler_params=params(),
        cost_estimate=cost(4 * offsets * rows * (halo + channels) * channels, 12e6),
    )(place, index16, first, local, stack)

    core = lax.axis_index("gc")
    half = 16 * channels
    steps = 9
    part = offsets // steps * channels
    activ, grad, mine, other = pl.pallas_call(
        point_kernel,
        grid=(steps,),
        out_shape=(
            jax.ShapeDtypeStruct((rows, channels), BF),
            jax.ShapeDtypeStruct((rows, channels), BF),
            jax.ShapeDtypeStruct((half, channels), BF),
            jax.ShapeDtypeStruct((half, channels), BF),
        ),
        in_specs=[
            SM,
            whole(channels, rows),
            whole(bricks * 32, channels),
            whole(1, rows),
            whole(channels, channels),
            whole(channels, 1),
            pl.BlockSpec((part, rows), lambda g: (g, 0)),
        ],
        out_specs=(
            whole(rows, channels),
            whole(rows, channels),
            whole(half, channels),
            whole(half, channels),
        ),
        compiler_params=params(),
    )(
        core.astype(jnp.int32)[None],
        conv,
        second.reshape(bricks * 32, channels),
        labels[0, 0, 0][None, :],
        ref_weight,
        cls_weight.astype(F32)[:, None],
        gathered,
    )

    got = lax.ppermute(other, "gc", [(0, 1), (1, 0)])
    chips = frames * lax.axis_size("gz") * ycount
    share = half // chips
    summed = (mine.astype(F32) + got.astype(F32)).astype(BF).reshape(chips, share, channels)
    summed = lax.all_to_all(summed, REST, split_axis=0, concat_axis=0, tiled=True)

    spread, low, mid, high = pl.pallas_call(
        lambda *refs: rim_grad_kernel(rows, *refs),
        grid=(groups,),
        out_shape=(
            jax.ShapeDtypeStruct((offsets * rows, channels), BF),
            jax.ShapeDtypeStruct((halo // 3, channels), BF),
            jax.ShapeDtypeStruct((halo // 3, channels), F32),
            jax.ShapeDtypeStruct((halo // 3, channels), BF),
        ),
        in_specs=[index_spec, whole(rows, channels), weight_spec],
        out_specs=(
            pl.BlockSpec((GROUP * rows, channels), lambda g: (g, 0)),
            whole(halo // 3, channels),
            whole(halo // 3, channels),
            whole(halo // 3, channels),
        ),
        scratch_shapes=[pltpu.VMEM((halo, channels), F32)],
        compiler_params=params(),
        cost_estimate=cost(4 * offsets * rows * (halo + channels) * channels, 6e6),
    )(index16, grad, stack)
    from_high = shifted(low, X, xcount, -1)
    from_low = shifted(high, X, xcount, 1)
    own = pl.pallas_call(
        own_grad_kernel,
        grid=(groups,),
        out_shape=jax.ShapeDtypeStruct((rows, channels), F32),
        in_specs=[index_spec, pl.BlockSpec((GROUP * rows, channels), lambda g: (g, 0))],
        out_specs=whole(rows, channels),
        compiler_params=params(),
        cost_estimate=cost(4 * offsets * rows * rows * channels, 6e6),
    )(index16, spread)
    column = mid + from_high.astype(F32) + from_low.astype(F32)
    from_right = shifted(column[0:rim].astype(BF), "gy", ycount, -1)
    from_left = shifted(column[2 * rim :].astype(BF), "gy", ycount, 1)
    feature_grad = pl.pallas_call(
        join_kernel,
        out_shape=jax.ShapeDtypeStruct((rows, channels), BF),
        in_specs=[VM] * 5,
        out_specs=VM,
        compiler_params=params(),
    )(
        own,
        column[rim : 2 * rim],
        from_right,
        from_left,
        jnp.pad(rim_index[None, :], ((0, 0), (0, LANES - rim))),
    )

    total = jnp.sum(summed.astype(F32), axis=0).astype(BF)
    total = jnp.broadcast_to(total[None], (chips, share, channels))
    total = lax.all_to_all(total, REST, split_axis=0, concat_axis=0, tiled=True)
    total = total.reshape(half, channels)
    partner = lax.ppermute(total, "gc", [(0, 1), (1, 0)])
    low_half = jnp.where(core == 0, total, partner).astype(F32)
    high_half = jnp.where(core == 0, partner, total).astype(F32)
    rest = offsets * channels - half
    weight_grad = jnp.concatenate([low_half, high_half[:rest]], axis=0)
    weight_grad = weight_grad.reshape(offsets, channels, channels)
    ref_grad = high_half[rest : rest + channels]
    return (activ[None, None, None], feature_grad[None, None, None], weight_grad, ref_grad)


def solution(mesh):
    frames, xcount, ycount = (mesh.shape[name] for name in ("ta", "gx", "gy"))
    fine = Mesh(
        mesh.devices.reshape(frames, xcount // 2, 2, ycount), ("ta", "gz", "gc", "gy")
    )
    three = P("ta", X, "gy", None)
    four = P("ta", X, "gy", None, None)
    placed = (four, four, three, four, four, three, three, three, P(), P(), P())
    return jax.shard_map(
        per_device,
        mesh=fine,
        in_specs=placed,
        out_specs=(four, four, P(), P()),
        check_vma=False,
    )
```

```python
import jax
import jax.numpy as jnp
from jax import lax
from jax.experimental import pallas as pl
from jax.experimental.pallas import tpu as pltpu
from jax.sharding import Mesh
from jax.sharding import PartitionSpec as P

BF = jnp.bfloat16
F32 = jnp.float32
I16 = jnp.int16
BLOCK = 128
LANES = 128
CAP = 2
GROUP = 9
LOSS_SCALE = 16.0
NT = (((1,), (1,)), ((), ()))
TN = (((0,), (0,)), ((), ()))
X = ("gz", "gc")
PLANE = ("gz", "gc", "gy")
REST = ("ta", "gz", "gy")


def params(mebibytes=16):
    return pltpu.CompilerParams(vmem_limit_bytes=mebibytes * 1024 * 1024)


def cost(flops, moved):
    return pl.CostEstimate(flops=int(flops), bytes_accessed=int(moved), transcendentals=0)


def iota(shape, dim):
    return lax.broadcasted_iota(jnp.int32, shape, dim)


def dot(left, right):
    return jnp.dot(left, right, preferred_element_type=F32)


def hot_of(mask):
    return jnp.where(mask, jnp.ones((), BF), jnp.zeros((), BF))


def lane_hot(column, width):
    n = column.shape[0]
    lane = iota((n, LANES), 1).astype(I16)
    column = column.astype(I16)
    pieces = []
    for start in range(0, width, LANES):
        piece = hot_of(column - jnp.asarray(start, I16) == lane)
        pieces.append(piece[:, : min(LANES, width - start)])
    return jnp.concatenate(pieces, axis=1) if len(pieces) > 1 else pieces[0]


def sublane_hot(row, start, height, width):
    base = iota((height, width), 0).astype(I16)
    rows = jnp.broadcast_to(row - start, (16, width)).astype(I16)
    wide = jnp.broadcast_to(rows[None], (height // 16, 16, width)).reshape(height, width)
    return hot_of(wide == base)


def list_kernel(blocks, lists_ref, counts_ref, source_ref, out_ref):
    dests = lists_ref.shape[1]
    lane = iota((dests, LANES), 1)
    dest = iota((dests, LANES), 0)
    row = jnp.zeros((1, LANES), F32)
    for c in range(CAP):
        listed = jnp.where(counts_ref[...] > c, lists_ref[c : c + 1, :], blocks).astype(F32)
        entry = jnp.broadcast_to(listed, (LANES, dests)).T
        row += jnp.sum(jnp.where(lane == dest * CAP + c, entry, 0.0), axis=0, keepdims=True)
    height = source_ref.shape[0]
    out_ref[0:height, :] = source_ref[...]
    first = iota((16, LANES), 0) == 0
    out_ref[height : height + 16, :] = jnp.where(first, row, 0.0).astype(BF)


def turn_kernel(current_ref, rim_ref, turned_ref, picked_ref):
    count = rim_ref.shape[1]
    turned = current_ref[...].T
    turned_ref[...] = turned
    hot = hot_of(iota((current_ref.shape[0], count), 0) == rim_ref[...])
    picked_ref[...] = dot(turned, hot).T.astype(BF)


def pack_kernel(blocks, match_ref, shift_ref, rim_ref, out_ref):
    bricks = out_ref.shape[0]
    step = BLOCK // bricks
    n = bricks * 32
    rows = iota((n, LANES), 0)
    i, j = rows // 32, rows % 32
    used = blocks * step
    target = jnp.where(
        j < used,
        (j // step) * BLOCK + i * step + j % step,
        jnp.where(j == used, blocks * BLOCK, -1),
    )
    hot = lane_hot(target, shift_ref.shape[0])
    out = dot(hot, shift_ref[...])
    wanted = jnp.broadcast_to(match_ref[...], (8, blocks)).astype(F32).astype(BF)
    slots = dot(wanted, hot_of(iota((blocks, LANES), 0) == iota((blocks, LANES), 1)))[0:1]
    out = jnp.where(j == used + 1, slots, out).astype(BF)
    out_ref[:, 0:32, :] = out.reshape(bricks, 32, LANES)
    count = rim_ref.shape[0]
    rim = rim_ref[...]
    for brick in range(bricks):
        out_ref[brick, 32 : 32 + count, :] = rim


def select_kernel(blocks, recv_ref, out_ref):
    bricks = out_ref.shape[0]
    step = BLOCK // bricks
    used = blocks * step
    n = bricks * 32
    tail = recv_ref[:, 16:32, :].astype(F32)
    which = iota(tail.shape, 1)
    coded = jnp.sum(jnp.where(which == used - 16, tail, 0.0), axis=1).astype(BF)
    slots = jnp.sum(jnp.where(which == used - 15, tail, 0.0), axis=1).astype(BF)
    rows = iota((n, LANES), 0)
    lane = iota((n, LANES), 1)
    d, j = rows // 32, rows % 32
    own = hot_of(d == lane)[:, :bricks]
    listed = dot(own, slots)
    slot = jnp.sum(jnp.where(lane == j // step, listed, 0.0), axis=1, keepdims=True)
    slot = jnp.broadcast_to(slot, (n, LANES)).astype(jnp.int32)
    entry = hot_of(lane == d * CAP + slot % CAP)
    codes = lax.dot_general(entry, coded, NT, preferred_element_type=F32)
    source = slot // CAP
    code = jnp.sum(
        jnp.where(lane[:, :bricks] == source[:, :bricks], codes, 0.0), axis=1, keepdims=True
    )
    code = jnp.broadcast_to(code, (n, LANES)).astype(jnp.int32)
    live = (slot < bricks * CAP) & (code < blocks) & (j < used)
    index = jnp.where(live, source * 32 + code * step + j % step, -1)
    data = recv_ref[:, 0:32, :].reshape(n, LANES)
    out_ref[...] = dot(lane_hot(index, n), data).astype(BF).reshape(out_ref.shape)


def local_kernel(idx_ref, turned_ref, out_ref):
    height, width = turned_ref.shape[1], out_ref.shape[1]
    for o in range(GROUP):
        hot = sublane_hot(idx_ref[o], 0, height, width)
        out_ref[o * LANES : (o + 1) * LANES, :] = dot(turned_ref[...], hot).astype(BF)


def halo_kernel(
    xcount, ycount, idx_ref, recv_ref, local_ref, w_ref, out_ref, conv_ref, turned_ref
):
    width = out_ref.shape[1]
    rim = recv_ref.shape[1] - 32

    @pl.when(pl.program_id(0) == 0)
    def _():
        conv_ref[...] = jnp.zeros_like(conv_ref)
        pieces = []
        for i in range(3):
            for j in range(3):
                a = lax.axis_index(X) + (i - 1)
                b = lax.axis_index("gy") + (j - 1)
                inside = (a >= 0) & (a < xcount) & (b >= 0) & (b < ycount)
                q = jnp.clip(a, 0, xcount - 1) * ycount + jnp.clip(b, 0, ycount - 1)
                piece = recv_ref[q, 32 : 32 + rim, :].astype(F32)
                pieces.append(jnp.where(inside, piece, 0.0))
        turned_ref[...] = jnp.concatenate(pieces, axis=0).astype(BF).T

    for o in range(GROUP):
        hot = sublane_hot(idx_ref[o], width, 9 * rim, width)
        part = dot(turned_ref[...], hot).astype(BF)
        span = slice(o * LANES, (o + 1) * LANES)
        out_ref[span, :] = local_ref[span, :] + part
    conv_ref[...] += lax.dot_general(w_ref[...], out_ref[...], TN, preferred_element_type=F32)


def point_kernel(
    conv_ref, recv_ref, label_ref, ref_w_ref, cls_ref, gathered_ref,
    activ_ref, turned_ref, mine_ref, other_ref, grad_ref,
):
    width = conv_ref.shape[1]
    core = lax.axis_index("gc")
    half = mine_ref.shape[0]
    step_id = pl.program_id(0)
    per_step = gathered_ref.shape[0]

    def put(first, value):
        into_mine = (first // half) == core
        at = pl.ds(pl.multiple_of(first % half, LANES), value.shape[0])

        @pl.when(into_mine)
        def _():
            mine_ref[at, :] = value

        @pl.when(jnp.logical_not(into_mine))
        def _():
            other_ref[at, :] = value

    @pl.when(step_id == 0)
    def _():
        mine_ref[...] = jnp.zeros_like(mine_ref)
        other_ref[...] = jnp.zeros_like(other_ref)
        bricks = recv_ref.shape[0] // 32
        step = BLOCK // bricks
        v = iota((1, width), 1)
        place = ((v % BLOCK) // step) * 32 + (v // BLOCK) * step + v % step
        hot = sublane_hot(place, 0, recv_ref.shape[0], width)
        matched = dot(recv_ref[...].T, hot).astype(BF)
        preact = conv_ref[...] + lax.dot_general(
            ref_w_ref[...], matched, TN, preferred_element_type=F32
        )
        cls = jnp.broadcast_to(cls_ref[...].astype(F32), (8, LANES)).T[:, 0:1]
        sig = jax.nn.sigmoid(preact)
        activ = (preact * sig).astype(BF)
        wide = activ.astype(F32)
        logits = jnp.sum(wide * cls, axis=0, keepdims=True)
        resid = jax.nn.sigmoid(logits) - label_ref[...].astype(F32)
        grad = LOSS_SCALE * resid * cls * sig * (1.0 + preact * (1.0 - sig))
        activ_ref[...] = wide.T.astype(BF)
        turned_ref[...] = grad.astype(BF)
        grad_ref[...] = grad.T.astype(BF)
        put(per_step * pl.num_programs(0), dot(matched, grad_ref[...]).astype(BF))

    terms = dot(gathered_ref[...], grad_ref[...]).astype(BF)
    for o in range(per_step // LANES):
        put(step_id * per_step + o * LANES, terms[o * LANES : (o + 1) * LANES])


def add_rows(start, piece, idx_ref, grad_ref, w_ref, acc_ref, spread_ref):
    width, height = grad_ref.shape[1], acc_ref.shape[1]
    parts = dot(w_ref[...], grad_ref[...]).astype(BF)
    for o in range(GROUP):
        spread_ref[:, o * width : (o + 1) * width] = parts[o * LANES : (o + 1) * LANES]
    rows = jnp.concatenate(
        [idx_ref[o] for o in range(GROUP)] + [jnp.zeros((16 - GROUP, width), jnp.int32)], axis=0
    )
    columns = (rows - start).T
    for first in range(0, height, piece):
        size = min(piece, height - first)
        hot = jnp.concatenate(
            [
                lane_hot(jnp.broadcast_to(columns[:, o : o + 1] - first, (width, LANES)), size)
                for o in range(GROUP)
            ],
            axis=0,
        )
        acc_ref[:, first : first + size] += dot(spread_ref[...], hot)


def rim_grad_kernel(
    start, idx_ref, grad_ref, w_ref, near_ref, mid_ref, far_ref, acc_ref, spread_ref
):
    @pl.when(pl.program_id(0) == 0)
    def _():
        acc_ref[...] = jnp.zeros_like(acc_ref)

    height = acc_ref.shape[1]
    add_rows(start, height, idx_ref, grad_ref, w_ref, acc_ref, spread_ref)

    @pl.when(pl.program_id(0) == pl.num_programs(0) - 1)
    def _():
        third = height // 3
        total = acc_ref[...].T
        even = lax.axis_index(X) % 2 == 0
        low = total[0:third].astype(BF)
        high = total[2 * third : 3 * third].astype(BF)
        near_ref[...] = jnp.where(even, high, low)
        mid_ref[...] = total[third : 2 * third]
        far_ref[...] = jnp.where(even, low, high)


def own_grad_kernel(
    idx_ref, grad_ref, w_ref, mid_ref, low_ref, high_ref, rim_ref, out_ref, acc_ref, spread_ref
):
    @pl.when(pl.program_id(0) == 0)
    def _():
        acc_ref[...] = jnp.zeros_like(acc_ref)

    add_rows(0, acc_ref.shape[1] // 2, idx_ref, grad_ref, w_ref, acc_ref, spread_ref)

    @pl.when(pl.program_id(0) == pl.num_programs(0) - 1)
    def _():
        total = mid_ref[...] + low_ref[...].astype(F32) + high_ref[...].astype(F32)
        upper = total.astype(BF)
        lower = (total - upper.astype(F32)).astype(BF)
        height, count = out_ref.shape[0], total.shape[0]
        hot = hot_of(iota((height, count), 0) == rim_ref[...])
        out_ref[...] = (acc_ref[...].T + dot(hot, upper) + dot(hot, lower)).astype(BF)


def column_kernel(mid_ref, near_in_ref, far_in_ref, near_ref, mine_ref, far_ref):
    total = mid_ref[...] + near_in_ref[...].astype(F32) + far_in_ref[...].astype(F32)
    third = total.shape[0] // 3
    even = lax.axis_index("gy") % 2 == 0
    low = total[0:third].astype(BF)
    high = total[2 * third : 3 * third].astype(BF)
    near_ref[...] = jnp.where(even, high, low)
    mine_ref[...] = total[third : 2 * third]
    far_ref[...] = jnp.where(even, low, high)


def sum_kernel(parts_ref, after_ref, out_ref):
    total = jnp.sum(parts_ref[...].astype(F32), axis=0).astype(BF)
    out_ref[...] = jnp.broadcast_to(total[None], out_ref.shape)


def finish_kernel(mine_ref, other_ref, weight_ref, ref_ref):
    core = lax.axis_index("gc")
    half = mine_ref.shape[0]
    rest = weight_ref.shape[0] - half
    tail = ref_ref.shape[0]

    def write(low_ref, high_ref):
        weight_ref[0:half, :] = low_ref[...].astype(F32)
        weight_ref[half : half + rest, :] = high_ref[0:rest, :].astype(F32)
        ref_ref[...] = high_ref[rest : rest + tail, :].astype(F32)

    @pl.when(core == 0)
    def _():
        write(mine_ref, other_ref)

    @pl.when(core != 0)
    def _():
        write(other_ref, mine_ref)


def shifted(block, axis, count, distance):
    route = [(i - distance, i) for i in range(count) if 0 <= i - distance < count]
    return lax.ppermute(block, axis, route)


def swapped(block, axis, count, start):
    route = []
    for i in range(start, count - 1, 2):
        route += [(i, i + 1), (i + 1, i)]
    return lax.ppermute(block, axis, route)


def per_device(
    feat,
    ref_feat,
    rim_rows,
    nbr,
    send_blocks,
    send_count,
    match_slot,
    labels,
    conv_weight,
    ref_weight,
    cls_weight,
):
    current = feat[0, 0, 0]
    rows, channels = current.shape
    blocks = rows // BLOCK
    rim = rim_rows.shape[3]
    offsets = nbr.shape[3]
    frames, ycount = lax.axis_size("ta"), lax.axis_size("gy")
    xcount = lax.axis_size(X)
    bricks = xcount * ycount
    halo = 9 * rim

    def whole(*shape):
        return pl.BlockSpec(shape, lambda g: (0,) * len(shape))

    def simple(kernel, shapes, *operands):
        shapes = [jax.ShapeDtypeStruct(*shape) for shape in shapes]
        specs = [whole(*shape.shape) for shape in shapes]
        one = len(shapes) == 1
        return pl.pallas_call(
            kernel,
            grid=(1,),
            out_shape=shapes[0] if one else shapes,
            in_specs=[whole(*operand.shape) for operand in operands],
            out_specs=specs[0] if one else specs,
            compiler_params=params(),
        )(*operands)

    def hbm(operand):
        return pltpu.with_memory_space_constraint(operand, pltpu.HBM)

    source = simple(
        lambda *refs: list_kernel(blocks, *refs),
        [((rows + 16, channels), BF)],
        hbm(send_blocks[0, 0, 0].T),
        hbm(send_count[0, 0]),
        hbm(ref_feat[0, 0, 0]),
    )
    source = shifted(source, "ta", frames, 1)
    turned, picked = simple(
        turn_kernel,
        [((channels, rows), BF), ((rim, channels), BF)],
        hbm(current),
        hbm(rim_rows[0, 0]),
    )
    packed = simple(
        lambda *refs: pack_kernel(blocks, *refs),
        [((bricks, 32 + rim, channels), BF)],
        hbm(match_slot[0, 0]),
        source,
        picked,
    )
    first = lax.all_to_all(packed, PLANE, split_axis=0, concat_axis=0, tiled=True)

    index = hbm(nbr.reshape(offsets, 1, rows))
    groups = offsets // GROUP
    stack = hbm(conv_weight.reshape(offsets * channels, channels))
    index_spec = pl.BlockSpec((GROUP, 1, rows), lambda g: (g, 0, 0))
    gather_spec = pl.BlockSpec((GROUP * channels, rows), lambda g: (g, 0))
    weight_spec = pl.BlockSpec((GROUP * channels, channels), lambda g: (g, 0))

    local = pl.pallas_call(
        local_kernel,
        grid=(groups,),
        out_shape=pltpu.HBM((offsets * channels, rows), BF),
        in_specs=[index_spec, whole(channels, rows)],
        out_specs=gather_spec,
        compiler_params=params(),
        cost_estimate=cost(4 * offsets * rows * rows * channels, 6e6),
    )(index, turned)

    chosen = simple(
        lambda *refs: select_kernel(blocks, *refs), [((bricks, 32, channels), BF)], first
    )
    second = lax.all_to_all(chosen, PLANE, split_axis=0, concat_axis=0, tiled=True)

    gathered, conv = pl.pallas_call(
        lambda *refs: halo_kernel(xcount, ycount, *refs),
        grid=(groups,),
        out_shape=(
            pltpu.HBM((offsets * channels, rows), BF),
            jax.ShapeDtypeStruct((channels, rows), F32),
        ),
        in_specs=[
            index_spec,
            whole(bricks, 32 + rim, channels),
            gather_spec,
            weight_spec,
        ],
        out_specs=(gather_spec, whole(channels, rows)),
        scratch_shapes=[pltpu.VMEM((channels, halo), BF)],
        compiler_params=params(),
        cost_estimate=cost(4 * offsets * rows * (halo + channels) * channels, 12e6),
    )(index, first, hbm(local), stack)

    half = 16 * channels
    steps = 3
    part = offsets // steps * channels
    activ, grad_turned, mine, other = pl.pallas_call(
        point_kernel,
        grid=(steps,),
        out_shape=(
            jax.ShapeDtypeStruct((rows, channels), BF),
            jax.ShapeDtypeStruct((channels, rows), BF),
            jax.ShapeDtypeStruct((half, channels), BF),
            jax.ShapeDtypeStruct((half, channels), BF),
        ),
        in_specs=[
            whole(channels, rows),
            whole(bricks * 32, channels),
            whole(1, rows),
            whole(channels, channels),
            whole(1, channels),
            pl.BlockSpec((part, rows), lambda g: (g, 0)),
        ],
        out_specs=(
            whole(rows, channels),
            whole(channels, rows),
            whole(half, channels),
            whole(half, channels),
        ),
        scratch_shapes=[pltpu.VMEM((rows, channels), BF)],
        compiler_params=params(),
    )(
        conv,
        second.reshape(bricks * 32, channels),
        hbm(labels[0, 0]),
        hbm(ref_weight),
        hbm(cls_weight[None, :]),
        hbm(gathered),
    )

    got = lax.ppermute(other, "gc", [(0, 1), (1, 0)])
    chips = frames * lax.axis_size("gz") * ycount
    share = half // chips
    summed = (mine.astype(F32) + got.astype(F32)).astype(BF).reshape(chips, share, channels)
    summed = lax.all_to_all(summed, REST, split_axis=0, concat_axis=0, tiled=True)

    third = halo // 3
    near, mid, far = pl.pallas_call(
        lambda *refs: rim_grad_kernel(rows, *refs),
        grid=(groups,),
        out_shape=(
            jax.ShapeDtypeStruct((third, channels), BF),
            jax.ShapeDtypeStruct((third, channels), F32),
            jax.ShapeDtypeStruct((third, channels), BF),
        ),
        in_specs=[index_spec, whole(channels, rows), weight_spec],
        out_specs=(whole(third, channels), whole(third, channels), whole(third, channels)),
        scratch_shapes=[
            pltpu.VMEM((channels, halo), F32),
            pltpu.VMEM((channels, GROUP * rows), BF),
        ],
        compiler_params=params(24),
        cost_estimate=cost(4 * offsets * rows * (halo + channels) * channels, 2e6),
    )(index, grad_turned, stack)
    near = swapped(near, X, xcount, 0)
    far = swapped(far, X, xcount, 1)
    third = (rim, channels)
    near, mid, far = simple(
        column_kernel, [(third, BF), (third, F32), (third, BF)], mid, near, far
    )
    total = simple(sum_kernel, [((chips, share, channels), BF)], summed, mid)
    total = lax.all_to_all(total, REST, split_axis=0, concat_axis=0, tiled=True)
    near = swapped(near, "gy", ycount, 0)
    far = swapped(far, "gy", ycount, 1)
    feature_grad = pl.pallas_call(
        own_grad_kernel,
        grid=(groups,),
        out_shape=jax.ShapeDtypeStruct((rows, channels), BF),
        in_specs=[index_spec, whole(channels, rows), weight_spec]
        + [whole(rim, channels)] * 3
        + [whole(1, rim)],
        out_specs=whole(rows, channels),
        scratch_shapes=[
            pltpu.VMEM((channels, rows), F32),
            pltpu.VMEM((channels, GROUP * rows), BF),
        ],
        compiler_params=params(24),
        cost_estimate=cost(4 * offsets * rows * rows * channels, 2e6),
    )(index, grad_turned, stack, mid, near, far, hbm(rim_rows[0, 0]))

    feature_grad, total = lax.optimization_barrier((feature_grad, total))
    total = total.reshape(half, channels)
    partner = lax.ppermute(total, "gc", [(0, 1), (1, 0)])
    weight_grad, ref_grad = simple(
        finish_kernel,
        [((offsets * channels, channels), F32), ((channels, channels), F32)],
        total,
        partner,
    )
    weight_grad = weight_grad.reshape(offsets, channels, channels)
    return (activ[None, None, None], feature_grad[None, None, None], weight_grad, ref_grad)


def solution(mesh):
    frames, xcount, ycount = (mesh.shape[name] for name in ("ta", "gx", "gy"))
    fine = Mesh(
        mesh.devices.reshape(frames, xcount // 2, 2, ycount), ("ta", "gz", "gc", "gy")
    )
    three = P("ta", X, "gy", None)
    four = P("ta", X, "gy", None, None)
    placed = (four, four, three, four, four, three, three, three, P(), P(), P())
    return jax.shard_map(
        per_device,
        mesh=fine,
        in_specs=placed,
        out_specs=(four, four, P(), P()),
        check_vma=False,
    )
```

```python
import jax
import jax.numpy as jnp
from jax import lax
from jax.experimental import pallas as pl
from jax.experimental.pallas import tpu as pltpu
from jax.sharding import Mesh
from jax.sharding import PartitionSpec as P

BF = jnp.bfloat16
F32 = jnp.float32
I16 = jnp.int16
BLOCK = 128
LANES = 128
CAP = 2
GROUP = 9
LOSS_SCALE = 16.0
NT = (((1,), (1,)), ((), ()))
TN = (((0,), (0,)), ((), ()))
X = ("gz", "gc")
PLANE = ("gz", "gc", "gy")
REST = ("ta", "gz", "gy")


def params(mebibytes=16):
    return pltpu.CompilerParams(vmem_limit_bytes=mebibytes * 1024 * 1024)


def cost(flops, moved):
    return pl.CostEstimate(flops=int(flops), bytes_accessed=int(moved), transcendentals=0)


def iota(shape, dim):
    return lax.broadcasted_iota(jnp.int32, shape, dim)


def dot(left, right):
    return jnp.dot(left, right, preferred_element_type=F32)


def hot_of(mask):
    return jnp.where(mask, jnp.ones((), BF), jnp.zeros((), BF))


def lane_hot(column, width):
    n = column.shape[0]
    lane = iota((n, LANES), 1).astype(I16)
    column = column.astype(I16)
    pieces = []
    for start in range(0, width, LANES):
        piece = hot_of(column - jnp.asarray(start, I16) == lane)
        pieces.append(piece[:, : min(LANES, width - start)])
    return jnp.concatenate(pieces, axis=1) if len(pieces) > 1 else pieces[0]


def sublane_hot(row, start, height, width):
    base = iota((height, width), 0).astype(I16)
    rows = jnp.broadcast_to(row - start, (16, width)).astype(I16)
    wide = jnp.broadcast_to(rows[None], (height // 16, 16, width)).reshape(height, width)
    return hot_of(wide == base)


def list_kernel(blocks, lists_ref, counts_ref, source_ref, out_ref):
    dests = lists_ref.shape[1]
    lane = iota((dests, LANES), 1)
    dest = iota((dests, LANES), 0)
    row = jnp.zeros((1, LANES), F32)
    for c in range(CAP):
        listed = jnp.where(counts_ref[...] > c, lists_ref[c : c + 1, :], blocks).astype(F32)
        entry = jnp.broadcast_to(listed, (LANES, dests)).T
        row += jnp.sum(jnp.where(lane == dest * CAP + c, entry, 0.0), axis=0, keepdims=True)
    height = source_ref.shape[0]
    out_ref[0:height, :] = source_ref[...]
    first = iota((16, LANES), 0) == 0
    out_ref[height : height + 16, :] = jnp.where(first, row, 0.0).astype(BF)


def turn_kernel(
    current_ref, rim_ref, idx_ref, w_ref, after_ref, turned_ref, picked_ref, idx_out, w_out
):
    idx_out[...] = idx_ref[...]
    w_out[...] = w_ref[...]
    count = rim_ref.shape[1]
    turned = current_ref[...].T
    turned_ref[...] = turned
    hot = hot_of(iota((current_ref.shape[0], count), 0) == rim_ref[...])
    picked_ref[...] = dot(turned, hot).T.astype(BF)


def pack_kernel(blocks, match_ref, shift_ref, out_ref):
    bricks = out_ref.shape[0]
    step = BLOCK // bricks
    n = bricks * 32
    rows = iota((n, LANES), 0)
    i, j = rows // 32, rows % 32
    used = blocks * step
    target = jnp.where(
        j < used,
        (j // step) * BLOCK + i * step + j % step,
        jnp.where(j == used, blocks * BLOCK, -1),
    )
    hot = lane_hot(target, shift_ref.shape[0])
    out = dot(hot, shift_ref[...])
    wanted = jnp.broadcast_to(match_ref[...], (8, blocks)).astype(F32).astype(BF)
    slots = dot(wanted, hot_of(iota((blocks, LANES), 0) == iota((blocks, LANES), 1)))[0:1]
    out = jnp.where(j == used + 1, slots, out).astype(BF)
    out_ref[...] = out.reshape(bricks, 32, LANES)


def select_kernel(blocks, recv_ref, out_ref):
    bricks = out_ref.shape[0]
    step = BLOCK // bricks
    used = blocks * step
    room = out_ref.shape[1]
    n = bricks * room
    tail = recv_ref[:, 16:32, :].astype(F32)
    which = iota(tail.shape, 1)
    coded = jnp.sum(jnp.where(which == used - 16, tail, 0.0), axis=1).astype(BF)
    slots = jnp.sum(jnp.where(which == used - 15, tail, 0.0), axis=1).astype(BF)
    rows = iota((n, LANES), 0)
    lane = iota((n, LANES), 1)
    d, j = rows // room, rows % room
    own = hot_of(d == lane)[:, :bricks]
    listed = dot(own, slots)
    slot = jnp.sum(jnp.where(lane == j // step, listed, 0.0), axis=1, keepdims=True)
    slot = jnp.broadcast_to(slot, (n, LANES)).astype(jnp.int32)
    entry = hot_of(lane == d * CAP + slot % CAP)
    codes = lax.dot_general(entry, coded, NT, preferred_element_type=F32)
    source = slot // CAP
    code = jnp.sum(
        jnp.where(lane[:, :bricks] == source[:, :bricks], codes, 0.0), axis=1, keepdims=True
    )
    code = jnp.broadcast_to(code, (n, LANES)).astype(jnp.int32)
    live = (slot < bricks * CAP) & (code < blocks) & (j < used)
    index = jnp.where(live, source * 32 + code * step + j % step, -1)
    data = recv_ref[...].reshape(bricks * 32, LANES)
    out_ref[...] = dot(lane_hot(index, bricks * 32), data).astype(BF).reshape(out_ref.shape)


def local_kernel(idx_ref, turned_ref, near_ref, rim_ref, far_ref, out_ref, rims_ref):
    @pl.when(pl.program_id(0) == 0)
    def _():
        count = rim_ref.shape[0]
        for n, part_ref in enumerate((near_ref, rim_ref, far_ref)):
            rims_ref[n * count : (n + 1) * count, :] = part_ref[...]

    height, width = turned_ref.shape[1], out_ref.shape[1]
    for o in range(GROUP):
        hot = sublane_hot(idx_ref[o], 0, height, width)
        out_ref[o * LANES : (o + 1) * LANES, :] = dot(turned_ref[...], hot).astype(BF)


def halo_kernel(
    idx_ref, rims_ref, near_ref, far_ref, local_ref, w_ref, out_ref, conv_ref, turned_ref
):
    width = out_ref.shape[1]
    rim = rims_ref.shape[0] // 3

    @pl.when(pl.program_id(0) == 0)
    def _():
        conv_ref[...] = jnp.zeros_like(conv_ref)
        pieces = []
        even_x = lax.axis_index(X) % 2 == 0
        even_y = lax.axis_index("gy") % 2 == 0
        for i in range(3):
            third = 1 if i == 1 else jnp.where(even_x == (i == 2), 0, 2)
            rows = pl.ds(pl.multiple_of(third * rim, 16), rim)
            near, far = near_ref[rows, :].astype(F32), far_ref[rows, :].astype(F32)
            pieces.append(jnp.where(even_y, far, near))
            pieces.append(rims_ref[rows, :].astype(F32))
            pieces.append(jnp.where(even_y, near, far))
        turned_ref[...] = jnp.concatenate(pieces, axis=0).astype(BF).T

    for o in range(GROUP):
        hot = sublane_hot(idx_ref[o], width, 9 * rim, width)
        part = dot(turned_ref[...], hot).astype(BF)
        span = slice(o * LANES, (o + 1) * LANES)
        out_ref[span, :] = local_ref[span, :] + part
    conv_ref[...] += lax.dot_general(w_ref[...], out_ref[...], TN, preferred_element_type=F32)


def point_kernel(
    conv_ref, recv_ref, label_ref, ref_w_ref, cls_ref, gathered_ref,
    activ_ref, turned_ref, mine_ref, other_ref, grad_ref, held_ref, sems,
):
    groups, part = held_ref.shape[0], held_ref.shape[1]
    copies = [
        pltpu.make_async_copy(
            gathered_ref.at[pl.ds(g * part, part)], held_ref.at[g], sems.at[g]
        )
        for g in range(groups)
    ]
    for copy in copies:
        copy.start()
    width = conv_ref.shape[1]
    core = lax.axis_index("gc")
    half = mine_ref.shape[0]

    def put(first, value):
        into_mine = (first // half) == core
        at = slice(first % half, first % half + value.shape[0])

        @pl.when(into_mine)
        def _():
            mine_ref[at, :] = value

        @pl.when(jnp.logical_not(into_mine))
        def _():
            other_ref[at, :] = value

    bricks, room = recv_ref.shape[0], recv_ref.shape[1]
    step = BLOCK // bricks
    v = iota((1, width), 1)
    place = ((v % BLOCK) // step) * room + (v // BLOCK) * step + v % step
    hot = sublane_hot(place, 0, bricks * room, width)
    matched = dot(recv_ref[...].reshape(bricks * room, LANES).T, hot).astype(BF)
    preact = conv_ref[...] + lax.dot_general(
        ref_w_ref[...], matched, TN, preferred_element_type=F32
    )
    cls = jnp.broadcast_to(cls_ref[...].astype(F32), (8, LANES)).T[:, 0:1]
    sig = jax.nn.sigmoid(preact)
    activ = (preact * sig).astype(BF)
    wide = activ.astype(F32)
    logits = jnp.sum(wide * cls, axis=0, keepdims=True)
    resid = jax.nn.sigmoid(logits) - label_ref[...].astype(F32)
    grad = LOSS_SCALE * resid * cls * sig * (1.0 + preact * (1.0 - sig))
    activ_ref[...] = activ.T
    turned_ref[...] = grad.astype(BF)
    grad_ref[...] = grad.astype(BF).T
    put(groups * part, dot(matched, grad_ref[...]).astype(BF))
    used = groups * part + LANES
    put(used, jnp.zeros((2 * half - used, LANES), BF))
    for g in range(groups):
        copies[g].wait()
        terms = dot(held_ref[g], grad_ref[...]).astype(BF)
        for o in range(part // LANES):
            put(g * part + o * LANES, terms[o * LANES : (o + 1) * LANES])


def add_rows(start, piece, idx_ref, grad_ref, w_ref, acc_ref, spread_ref):
    width, height = grad_ref.shape[1], acc_ref.shape[1]
    parts = dot(w_ref[...], grad_ref[...]).astype(BF)
    for o in range(GROUP):
        spread_ref[:, o * width : (o + 1) * width] = parts[o * LANES : (o + 1) * LANES]
    rows = jnp.concatenate(
        [idx_ref[o] for o in range(GROUP)] + [jnp.zeros((16 - GROUP, width), jnp.int32)], axis=0
    )
    columns = (rows - start).T
    for first in range(0, height, piece):
        size = min(piece, height - first)
        hot = jnp.concatenate(
            [
                lane_hot(jnp.broadcast_to(columns[:, o : o + 1] - first, (width, LANES)), size)
                for o in range(GROUP)
            ],
            axis=0,
        )
        acc_ref[:, first : first + size] += dot(spread_ref[...], hot)


def grad_kernel(
    piece, idx_ref, grad_ref, w_ref, own_ref, near_ref, mid_ref, far_ref, acc_ref, spread_ref
):
    @pl.when(pl.program_id(0) == 0)
    def _():
        acc_ref[...] = jnp.zeros_like(acc_ref)

    add_rows(0, piece, idx_ref, grad_ref, w_ref, acc_ref, spread_ref)

    @pl.when(pl.program_id(0) == pl.num_programs(0) - 1)
    def _():
        own, third = own_ref.shape[0], near_ref.shape[0]
        total = acc_ref[...].T
        even = lax.axis_index(X) % 2 == 0
        low = total[own : own + third].astype(BF)
        high = total[own + 2 * third : own + 3 * third].astype(BF)
        own_ref[...] = total[0:own]
        near_ref[...] = jnp.where(even, high, low)
        mid_ref[...] = total[own + third : own + 2 * third]
        far_ref[...] = jnp.where(even, low, high)


def join_kernel(own_ref, mid_ref, low_ref, high_ref, rim_ref, out_ref):
    total = mid_ref[...] + low_ref[...].astype(F32) + high_ref[...].astype(F32)
    upper = total.astype(BF)
    lower = (total - upper.astype(F32)).astype(BF)
    height, count = out_ref.shape[0], total.shape[0]
    hot = hot_of(iota((height, count), 0) == rim_ref[...])
    out_ref[...] = (own_ref[...] + dot(hot, upper) + dot(hot, lower)).astype(BF)


def column_kernel(mid_ref, near_in_ref, far_in_ref, near_ref, mine_ref, far_ref):
    total = mid_ref[...] + near_in_ref[...].astype(F32) + far_in_ref[...].astype(F32)
    third = total.shape[0] // 3
    even = lax.axis_index("gy") % 2 == 0
    low = total[0:third].astype(BF)
    high = total[2 * third : 3 * third].astype(BF)
    near_ref[...] = jnp.where(even, high, low)
    mine_ref[...] = total[third : 2 * third]
    far_ref[...] = jnp.where(even, low, high)


def sum_kernel(parts_ref, after_ref, out_ref):
    total = jnp.sum(parts_ref[...].astype(F32), axis=0).astype(BF)
    out_ref[...] = jnp.broadcast_to(total[None], out_ref.shape)


def finish_kernel(mine_ref, other_ref, weight_ref, ref_ref):
    core = lax.axis_index("gc")
    half = mine_ref.shape[0]
    rest = weight_ref.shape[0] - half
    tail = ref_ref.shape[0]

    def write(low_ref, high_ref):
        weight_ref[0:half, :] = low_ref[...].astype(F32)
        weight_ref[half : half + rest, :] = high_ref[0:rest, :].astype(F32)
        ref_ref[...] = high_ref[rest : rest + tail, :].astype(F32)

    @pl.when(core == 0)
    def _():
        write(mine_ref, other_ref)

    @pl.when(core != 0)
    def _():
        write(other_ref, mine_ref)


def shifted(block, axis, count, distance):
    route = [(i - distance, i) for i in range(count) if 0 <= i - distance < count]
    return lax.ppermute(block, axis, route)


def swapped(block, axis, count, start):
    route = []
    for i in range(start, count - 1, 2):
        route += [(i, i + 1), (i + 1, i)]
    return lax.ppermute(block, axis, route)


def per_device(
    feat,
    ref_feat,
    rim_rows,
    nbr,
    send_blocks,
    send_count,
    match_slot,
    labels,
    conv_weight,
    ref_weight,
    cls_weight,
):
    current = feat[0, 0, 0]
    rows, channels = current.shape
    blocks = rows // BLOCK
    rim = rim_rows.shape[3]
    offsets = nbr.shape[3]
    frames, ycount = lax.axis_size("ta"), lax.axis_size("gy")
    xcount = lax.axis_size(X)
    bricks = xcount * ycount
    halo = 9 * rim

    def whole(*shape):
        return pl.BlockSpec(shape, lambda g: (0,) * len(shape))

    def simple(kernel, shapes, *operands):
        shapes = [jax.ShapeDtypeStruct(*shape) for shape in shapes]
        specs = [whole(*shape.shape) for shape in shapes]
        one = len(shapes) == 1
        return pl.pallas_call(
            kernel,
            grid=(1,),
            out_shape=shapes[0] if one else shapes,
            in_specs=[whole(*operand.shape) for operand in operands],
            out_specs=specs[0] if one else specs,
            compiler_params=params(),
        )(*operands)

    def hbm(operand):
        return pltpu.with_memory_space_constraint(operand, pltpu.HBM)

    source = simple(
        lambda *refs: list_kernel(blocks, *refs),
        [((rows + 16, channels), BF)],
        hbm(send_blocks[0, 0, 0].T),
        hbm(send_count[0, 0]),
        hbm(ref_feat[0, 0, 0]),
    )
    turn_shapes = [
        jax.ShapeDtypeStruct((channels, rows), BF),
        jax.ShapeDtypeStruct((rim, channels), BF),
        jax.ShapeDtypeStruct((offsets, 1, rows), jnp.int32),
        jax.ShapeDtypeStruct((offsets * channels, channels), BF),
    ]
    turn_inputs = [
        hbm(current),
        hbm(rim_rows[0, 0]),
        hbm(nbr.reshape(offsets, 1, rows)),
        hbm(conv_weight.reshape(offsets * channels, channels)),
    ]
    turned, picked, index, stack = pl.pallas_call(
        turn_kernel,
        grid=(1,),
        out_shape=turn_shapes,
        in_specs=[whole(*operand.shape) for operand in turn_inputs]
        + [pl.BlockSpec(memory_space=pl.ANY)],
        out_specs=[whole(*shape.shape) for shape in turn_shapes],
        compiler_params=params(),
    )(*turn_inputs, source)
    source = shifted(source, "ta", frames, 1)
    near_rim = swapped(picked, X, xcount, 0)
    far_rim = swapped(picked, X, xcount, 1)
    packed = simple(
        lambda *refs: pack_kernel(blocks, *refs),
        [((bricks, 32, channels), BF)],
        hbm(match_slot[0, 0]),
        source,
    )
    first = lax.all_to_all(packed, PLANE, split_axis=0, concat_axis=0, tiled=True)

    groups = offsets // GROUP
    index_spec = pl.BlockSpec((GROUP, 1, rows), lambda g: (g, 0, 0))
    gather_spec = pl.BlockSpec((GROUP * channels, rows), lambda g: (g, 0))
    weight_spec = pl.BlockSpec((GROUP * channels, channels), lambda g: (g, 0))

    local, rims = pl.pallas_call(
        local_kernel,
        grid=(groups,),
        out_shape=(
            pltpu.HBM((offsets * channels, rows), BF),
            jax.ShapeDtypeStruct((3 * rim, channels), BF),
        ),
        in_specs=[index_spec, whole(channels, rows)] + [whole(rim, channels)] * 3,
        out_specs=(gather_spec, whole(3 * rim, channels)),
        compiler_params=params(),
        cost_estimate=cost(4 * offsets * rows * rows * channels, 6e6),
    )(index, turned, near_rim, picked, far_rim)
    near_rims = swapped(rims, "gy", ycount, 0)
    far_rims = swapped(rims, "gy", ycount, 1)

    chosen = simple(
        lambda *refs: select_kernel(blocks, *refs), [((bricks, 24, channels), BF)], first
    )
    second = lax.all_to_all(chosen, PLANE, split_axis=0, concat_axis=0, tiled=True)

    gathered, conv = pl.pallas_call(
        halo_kernel,
        grid=(groups,),
        out_shape=(
            pltpu.HBM((offsets * channels, rows), BF),
            jax.ShapeDtypeStruct((channels, rows), F32),
        ),
        in_specs=[
            index_spec,
            whole(3 * rim, channels),
            whole(3 * rim, channels),
            whole(3 * rim, channels),
            gather_spec,
            weight_spec,
        ],
        out_specs=(gather_spec, whole(channels, rows)),
        scratch_shapes=[pltpu.VMEM((channels, halo), BF)],
        compiler_params=params(),
        cost_estimate=cost(4 * offsets * rows * (halo + channels) * channels, 12e6),
    )(index, rims, near_rims, far_rims, hbm(local), stack)

    half = 16 * channels
    part = offsets // groups * channels
    activ, grad_turned, mine, other = pl.pallas_call(
        point_kernel,
        grid=(1,),
        out_shape=(
            jax.ShapeDtypeStruct((rows, channels), BF),
            jax.ShapeDtypeStruct((channels, rows), BF),
            jax.ShapeDtypeStruct((half, channels), BF),
            jax.ShapeDtypeStruct((half, channels), BF),
        ),
        in_specs=[
            whole(channels, rows),
            whole(bricks, 24, channels),
            whole(1, rows),
            whole(channels, channels),
            whole(1, channels),
            pl.BlockSpec(memory_space=pl.ANY),
        ],
        out_specs=(
            whole(rows, channels),
            whole(channels, rows),
            whole(half, channels),
            whole(half, channels),
        ),
        scratch_shapes=[
            pltpu.VMEM((rows, channels), BF),
            pltpu.VMEM((groups, part, rows), BF),
            pltpu.SemaphoreType.DMA((groups,)),
        ],
        compiler_params=params(24),
    )(
        conv,
        second,
        hbm(labels[0, 0]),
        hbm(ref_weight),
        hbm(cls_weight[None, :]),
        hbm(gathered),
    )

    got = lax.ppermute(other, "gc", [(0, 1), (1, 0)])
    chips = frames * lax.axis_size("gz") * ycount
    share = half // chips
    summed = (mine.astype(F32) + got.astype(F32)).astype(BF).reshape(chips, share, channels)
    summed = lax.all_to_all(summed, REST, split_axis=0, concat_axis=0, tiled=True)

    third = (halo // 3, channels)
    own, near, mid, far = pl.pallas_call(
        lambda *refs: grad_kernel(768, *refs),
        grid=(groups,),
        out_shape=(
            jax.ShapeDtypeStruct((rows, channels), F32),
            jax.ShapeDtypeStruct(third, BF),
            jax.ShapeDtypeStruct(third, F32),
            jax.ShapeDtypeStruct(third, BF),
        ),
        in_specs=[index_spec, whole(channels, rows), weight_spec],
        out_specs=(whole(rows, channels), whole(*third), whole(*third), whole(*third)),
        scratch_shapes=[
            pltpu.VMEM((channels, rows + halo), F32),
            pltpu.VMEM((channels, GROUP * rows), BF),
        ],
        compiler_params=params(32),
        cost_estimate=cost(4 * offsets * rows * (rows + halo) * channels, 4e6),
    )(index, grad_turned, stack)
    total = simple(sum_kernel, [((chips, share, channels), BF)], summed, mid)
    total = lax.all_to_all(total, REST, split_axis=0, concat_axis=0, tiled=True)
    near = swapped(near, X, xcount, 0)
    far = swapped(far, X, xcount, 1)
    third = (rim, channels)
    near, mid, far = simple(
        column_kernel, [(third, BF), (third, F32), (third, BF)], mid, near, far
    )
    near = swapped(near, "gy", ycount, 0)
    far = swapped(far, "gy", ycount, 1)
    feature_grad = simple(
        join_kernel, [((rows, channels), BF)], own, mid, near, far, hbm(rim_rows[0, 0])
    )
    feature_grad, total = lax.optimization_barrier((feature_grad, total))
    total = total.reshape(half, channels)
    partner = lax.ppermute(total, "gc", [(0, 1), (1, 0)])
    weight_grad, ref_grad = simple(
        finish_kernel,
        [((offsets * channels, channels), F32), ((channels, channels), F32)],
        total,
        partner,
    )
    weight_grad = weight_grad.reshape(offsets, channels, channels)
    return (activ[None, None, None], feature_grad[None, None, None], weight_grad, ref_grad)


def solution(mesh):
    frames, xcount, ycount = (mesh.shape[name] for name in ("ta", "gx", "gy"))
    fine = Mesh(
        mesh.devices.reshape(frames, xcount // 2, 2, ycount), ("ta", "gz", "gc", "gy")
    )
    three = P("ta", X, "gy", None)
    four = P("ta", X, "gy", None, None)
    placed = (four, four, three, four, four, three, three, three, P(), P(), P())
    return jax.shard_map(
        per_device,
        mesh=fine,
        in_specs=placed,
        out_specs=(four, four, P(), P()),
        check_vma=False,
    )
```

```python
import jax
import jax.numpy as jnp
from jax import lax
from jax.experimental import pallas as pl
from jax.experimental.pallas import tpu as pltpu
from jax.sharding import Mesh
from jax.sharding import PartitionSpec as P

BF = jnp.bfloat16
F32 = jnp.float32
I16 = jnp.int16
BLOCK = 128
LANES = 128
CAP = 2
GROUP = 9
LOSS_SCALE = 16.0
NT = (((1,), (1,)), ((), ()))
TN = (((0,), (0,)), ((), ()))
X = ("gz", "gc")
PLANE = ("gz", "gc", "gy")
REST = ("ta", "gz", "gy")


def params(mebibytes=16):
    return pltpu.CompilerParams(vmem_limit_bytes=mebibytes * 1024 * 1024)


def cost(flops, moved):
    return pl.CostEstimate(flops=int(flops), bytes_accessed=int(moved), transcendentals=0)


def iota(shape, dim):
    return lax.broadcasted_iota(jnp.int32, shape, dim)


def dot(left, right):
    return jnp.dot(left, right, preferred_element_type=F32)


def hot_of(mask):
    return jnp.where(mask, jnp.ones((), BF), jnp.zeros((), BF))


def lane_hot(column, width):
    n = column.shape[0]
    lane = iota((n, LANES), 1).astype(I16)
    column = column.astype(I16)
    pieces = []
    for start in range(0, width, LANES):
        piece = hot_of(column - jnp.asarray(start, I16) == lane)
        pieces.append(piece[:, : min(LANES, width - start)])
    return jnp.concatenate(pieces, axis=1) if len(pieces) > 1 else pieces[0]


def sublane_hot(row, start, height, width):
    base = iota((height, width), 0).astype(I16)
    rows = jnp.broadcast_to(row - start, (16, width)).astype(I16)
    wide = jnp.broadcast_to(rows[None], (height // 16, 16, width)).reshape(height, width)
    return hot_of(wide == base)


def list_kernel(blocks, lists_ref, counts_ref, source_ref, out_ref):
    dests = lists_ref.shape[1]
    lane = iota((dests, LANES), 1)
    dest = iota((dests, LANES), 0)
    row = jnp.zeros((1, LANES), F32)
    for c in range(CAP):
        listed = jnp.where(counts_ref[...] > c, lists_ref[c : c + 1, :], blocks).astype(F32)
        entry = jnp.broadcast_to(listed, (LANES, dests)).T
        row += jnp.sum(jnp.where(lane == dest * CAP + c, entry, 0.0), axis=0, keepdims=True)
    height = source_ref.shape[0]
    out_ref[0:height, :] = source_ref[...]
    first = iota((16, LANES), 0) == 0
    out_ref[height : height + 16, :] = jnp.where(first, row, 0.0).astype(BF)


def turn_kernel(
    current_ref, rim_ref, idx_ref, w_ref, after_ref, turned_ref, picked_ref, idx_out, w_out
):
    idx_out[...] = idx_ref[...]
    w_out[...] = w_ref[...]
    count = rim_ref.shape[1]
    turned = current_ref[...].T
    turned_ref[...] = turned
    hot = hot_of(iota((current_ref.shape[0], count), 0) == rim_ref[...])
    picked_ref[...] = dot(turned, hot).T.astype(BF)


def pack_kernel(blocks, match_ref, shift_ref, out_ref):
    bricks = out_ref.shape[0]
    step = BLOCK // bricks
    n = bricks * 32
    rows = iota((n, LANES), 0)
    i, j = rows // 32, rows % 32
    used = blocks * step
    target = jnp.where(
        j < used,
        (j // step) * BLOCK + i * step + j % step,
        jnp.where(j == used, blocks * BLOCK, -1),
    )
    hot = lane_hot(target, shift_ref.shape[0])
    out = dot(hot, shift_ref[...])
    wanted = jnp.broadcast_to(match_ref[...], (8, blocks)).astype(F32).astype(BF)
    slots = dot(wanted, hot_of(iota((blocks, LANES), 0) == iota((blocks, LANES), 1)))[0:1]
    out = jnp.where(j == used + 1, slots, out).astype(BF)
    out_ref[...] = out.reshape(bricks, 32, LANES)


def select_kernel(blocks, recv_ref, out_ref):
    bricks = out_ref.shape[0]
    step = BLOCK // bricks
    used = blocks * step
    room = out_ref.shape[1]
    n = bricks * room
    tail = recv_ref[:, 16:32, :].astype(F32)
    which = iota(tail.shape, 1)
    coded = jnp.sum(jnp.where(which == used - 16, tail, 0.0), axis=1).astype(BF)
    slots = jnp.sum(jnp.where(which == used - 15, tail, 0.0), axis=1).astype(BF)
    rows = iota((n, LANES), 0)
    lane = iota((n, LANES), 1)
    d, j = rows // room, rows % room
    own = hot_of(d == lane)[:, :bricks]
    listed = dot(own, slots)
    slot = jnp.sum(jnp.where(lane == j // step, listed, 0.0), axis=1, keepdims=True)
    slot = jnp.broadcast_to(slot, (n, LANES)).astype(jnp.int32)
    entry = hot_of(lane == d * CAP + slot % CAP)
    codes = lax.dot_general(entry, coded, NT, preferred_element_type=F32)
    source = slot // CAP
    code = jnp.sum(
        jnp.where(lane[:, :bricks] == source[:, :bricks], codes, 0.0), axis=1, keepdims=True
    )
    code = jnp.broadcast_to(code, (n, LANES)).astype(jnp.int32)
    live = (slot < bricks * CAP) & (code < blocks) & (j < used)
    index = jnp.where(live, source * 32 + code * step + j % step, -1)
    data = recv_ref[...].reshape(bricks * 32, LANES)
    out_ref[...] = dot(lane_hot(index, bricks * 32), data).astype(BF).reshape(out_ref.shape)


def local_kernel(
    idx_ref, turned_ref, near_ref, rim_ref, far_ref, away_ref, kept_ref, rims_ref, held_ref, sems
):
    count = rim_ref.shape[0]
    for n, part_ref in enumerate((near_ref, rim_ref, far_ref)):
        rims_ref[n * count : (n + 1) * count, :] = part_ref[...]
    height, width = turned_ref.shape[1], kept_ref.shape[1]
    part = kept_ref.shape[0]
    copies = []
    for g in range(idx_ref.shape[0] // GROUP):
        target = held_ref.at[g] if g < held_ref.shape[0] else kept_ref
        for o in range(GROUP):
            hot = sublane_hot(idx_ref[g * GROUP + o], 0, height, width)
            target[o * LANES : (o + 1) * LANES, :] = dot(turned_ref[...], hot).astype(BF)
        if g < held_ref.shape[0]:
            copy = pltpu.make_async_copy(
                held_ref.at[g], away_ref.at[pl.ds(g * part, part)], sems.at[g]
            )
            copy.start()
            copies.append(copy)
    for copy in copies:
        copy.wait()


def halo_kernel(
    idx_ref, rims_ref, near_ref, far_ref, w_ref, kept_in_ref, away_in_ref,
    away_ref, kept_ref, conv_ref, turned_ref, held_ref, in_sems, out_sems,
):
    width, part = kept_ref.shape[1], kept_ref.shape[0]
    rim = rims_ref.shape[0] // 3
    fetches = [
        pltpu.make_async_copy(
            away_in_ref.at[pl.ds(g * part, part)], held_ref.at[g], in_sems.at[g]
        )
        for g in range(2)
    ]
    for fetch in fetches:
        fetch.start()
    pieces = []
    even_x = lax.axis_index(X) % 2 == 0
    even_y = lax.axis_index("gy") % 2 == 0
    for i in range(3):
        third = 1 if i == 1 else jnp.where(even_x == (i == 2), 0, 2)
        rows = pl.ds(pl.multiple_of(third * rim, 16), rim)
        near, far = near_ref[rows, :].astype(F32), far_ref[rows, :].astype(F32)
        pieces.append(jnp.where(even_y, far, near))
        pieces.append(rims_ref[rows, :].astype(F32))
        pieces.append(jnp.where(even_y, near, far))
    turned_ref[...] = jnp.concatenate(pieces, axis=0).astype(BF).T
    stores = []
    for n, g in enumerate((2, 0, 1)):
        if n > 0:
            fetches[g].wait()
        source = kept_in_ref if n == 0 else held_ref.at[g]
        target = kept_ref if n == 2 else held_ref.at[2 - 2 * n]
        for o in range(GROUP):
            hot = sublane_hot(idx_ref[g * GROUP + o], width, 9 * rim, width)
            value = dot(turned_ref[...], hot).astype(BF)
            span = slice(o * LANES, (o + 1) * LANES)
            target[span, :] = source[span, :] + value
        weight = w_ref[g * part : (g + 1) * part, :]
        term = lax.dot_general(weight, target[...], TN, preferred_element_type=F32)
        conv_ref[...] = term if n == 0 else conv_ref[...] + term
        if n < 2:
            store = pltpu.make_async_copy(
                target, away_ref.at[pl.ds(n * part, part)], out_sems.at[n]
            )
            store.start()
            stores.append(store)
    for store in stores:
        store.wait()


def point_kernel(
    conv_ref, recv_ref, label_ref, ref_w_ref, cls_ref, kept_ref, away_ref,
    activ_ref, turned_ref, mine_ref, other_ref, grad_ref, held_ref, sems,
):
    groups, part = held_ref.shape[0] + 1, held_ref.shape[1]
    copies = [
        pltpu.make_async_copy(
            away_ref.at[pl.ds(n * part, part)], held_ref.at[n], sems.at[n]
        )
        for n in range(groups - 1)
    ]
    for copy in copies:
        copy.start()
    width = conv_ref.shape[1]
    core = lax.axis_index("gc")
    half = mine_ref.shape[0]

    def put(first, value):
        into_mine = (first // half) == core
        at = slice(first % half, first % half + value.shape[0])

        @pl.when(into_mine)
        def _():
            mine_ref[at, :] = value

        @pl.when(jnp.logical_not(into_mine))
        def _():
            other_ref[at, :] = value

    bricks, room = recv_ref.shape[0], recv_ref.shape[1]
    step = BLOCK // bricks
    v = iota((1, width), 1)
    place = ((v % BLOCK) // step) * room + (v // BLOCK) * step + v % step
    hot = sublane_hot(place, 0, bricks * room, width)
    matched = dot(recv_ref[...].reshape(bricks * room, LANES).T, hot).astype(BF)
    preact = conv_ref[...] + lax.dot_general(
        ref_w_ref[...], matched, TN, preferred_element_type=F32
    )
    cls = jnp.broadcast_to(cls_ref[...].astype(F32), (8, LANES)).T[:, 0:1]
    sig = jax.nn.sigmoid(preact)
    activ = (preact * sig).astype(BF)
    wide = activ.astype(F32)
    logits = jnp.sum(wide * cls, axis=0, keepdims=True)
    resid = jax.nn.sigmoid(logits) - label_ref[...].astype(F32)
    grad = LOSS_SCALE * resid * cls * sig * (1.0 + preact * (1.0 - sig))
    activ_ref[...] = activ.T
    turned_ref[...] = grad.astype(BF)
    grad_ref[...] = grad.astype(BF).T
    put(groups * part, dot(matched, grad_ref[...]).astype(BF))
    used = groups * part + LANES
    put(used, jnp.zeros((2 * half - used, LANES), BF))
    for n, g in enumerate((1, 2, 0)):
        if n > 0:
            copies[n - 1].wait()
        held = kept_ref[...] if n == 0 else held_ref[n - 1]
        terms = dot(held, grad_ref[...]).astype(BF)
        for o in range(part // LANES):
            put(g * part + o * LANES, terms[o * LANES : (o + 1) * LANES])


def add_rows(start, piece, idx_ref, grad_ref, w_ref, acc_ref, spread_ref):
    width, height = grad_ref.shape[1], acc_ref.shape[1]
    parts = dot(w_ref[...], grad_ref[...]).astype(BF)
    for o in range(GROUP):
        spread_ref[:, o * width : (o + 1) * width] = parts[o * LANES : (o + 1) * LANES]
    rows = jnp.concatenate(
        [idx_ref[o] for o in range(GROUP)] + [jnp.zeros((16 - GROUP, width), jnp.int32)], axis=0
    )
    columns = (rows - start).T
    for first in range(0, height, piece):
        size = min(piece, height - first)
        hot = jnp.concatenate(
            [
                lane_hot(jnp.broadcast_to(columns[:, o : o + 1] - first, (width, LANES)), size)
                for o in range(GROUP)
            ],
            axis=0,
        )
        acc_ref[:, first : first + size] += dot(spread_ref[...], hot)


def grad_kernel(
    piece, idx_ref, grad_ref, w_ref, own_ref, near_ref, mid_ref, far_ref, acc_ref, spread_ref
):
    @pl.when(pl.program_id(0) == 0)
    def _():
        acc_ref[...] = jnp.zeros_like(acc_ref)

    add_rows(0, piece, idx_ref, grad_ref, w_ref, acc_ref, spread_ref)

    @pl.when(pl.program_id(0) == pl.num_programs(0) - 1)
    def _():
        own, third = own_ref.shape[0], near_ref.shape[0]
        total = acc_ref[...].T
        even = lax.axis_index(X) % 2 == 0
        low = total[own : own + third].astype(BF)
        high = total[own + 2 * third : own + 3 * third].astype(BF)
        own_ref[...] = total[0:own]
        near_ref[...] = jnp.where(even, high, low)
        mid_ref[...] = total[own + third : own + 2 * third]
        far_ref[...] = jnp.where(even, low, high)


def join_kernel(own_ref, mid_ref, low_ref, high_ref, rim_ref, out_ref):
    total = mid_ref[...] + low_ref[...].astype(F32) + high_ref[...].astype(F32)
    upper = total.astype(BF)
    lower = (total - upper.astype(F32)).astype(BF)
    height, count = out_ref.shape[0], total.shape[0]
    hot = hot_of(iota((height, count), 0) == rim_ref[...])
    out_ref[...] = (own_ref[...] + dot(hot, upper) + dot(hot, lower)).astype(BF)


def column_kernel(mid_ref, near_in_ref, far_in_ref, near_ref, mine_ref, far_ref):
    total = mid_ref[...] + near_in_ref[...].astype(F32) + far_in_ref[...].astype(F32)
    third = total.shape[0] // 3
    even = lax.axis_index("gy") % 2 == 0
    low = total[0:third].astype(BF)
    high = total[2 * third : 3 * third].astype(BF)
    near_ref[...] = jnp.where(even, high, low)
    mine_ref[...] = total[third : 2 * third]
    far_ref[...] = jnp.where(even, low, high)


def sum_kernel(parts_ref, after_ref, out_ref):
    total = jnp.sum(parts_ref[...].astype(F32), axis=0).astype(BF)
    out_ref[...] = jnp.broadcast_to(total[None], out_ref.shape)


def finish_kernel(mine_ref, other_ref, weight_ref, ref_ref):
    core = lax.axis_index("gc")
    half = mine_ref.shape[0]
    rest = weight_ref.shape[0] - half
    tail = ref_ref.shape[0]

    def write(low_ref, high_ref):
        weight_ref[0:half, :] = low_ref[...].astype(F32)
        weight_ref[half : half + rest, :] = high_ref[0:rest, :].astype(F32)
        ref_ref[...] = high_ref[rest : rest + tail, :].astype(F32)

    @pl.when(core == 0)
    def _():
        write(mine_ref, other_ref)

    @pl.when(core != 0)
    def _():
        write(other_ref, mine_ref)


def shifted(block, axis, count, distance):
    route = [(i - distance, i) for i in range(count) if 0 <= i - distance < count]
    return lax.ppermute(block, axis, route)


def swapped(block, axis, count, start):
    route = []
    for i in range(start, count - 1, 2):
        route += [(i, i + 1), (i + 1, i)]
    return lax.ppermute(block, axis, route)


def per_device(
    feat,
    ref_feat,
    rim_rows,
    nbr,
    send_blocks,
    send_count,
    match_slot,
    labels,
    conv_weight,
    ref_weight,
    cls_weight,
):
    current = feat[0, 0, 0]
    rows, channels = current.shape
    blocks = rows // BLOCK
    rim = rim_rows.shape[3]
    offsets = nbr.shape[3]
    frames, ycount = lax.axis_size("ta"), lax.axis_size("gy")
    xcount = lax.axis_size(X)
    bricks = xcount * ycount
    halo = 9 * rim

    def whole(*shape):
        return pl.BlockSpec(shape, lambda g: (0,) * len(shape))

    def simple(kernel, shapes, *operands):
        shapes = [jax.ShapeDtypeStruct(*shape) for shape in shapes]
        specs = [whole(*shape.shape) for shape in shapes]
        one = len(shapes) == 1
        return pl.pallas_call(
            kernel,
            grid=(1,),
            out_shape=shapes[0] if one else shapes,
            in_specs=[whole(*operand.shape) for operand in operands],
            out_specs=specs[0] if one else specs,
            compiler_params=params(),
        )(*operands)

    def hbm(operand):
        return pltpu.with_memory_space_constraint(operand, pltpu.HBM)

    source = simple(
        lambda *refs: list_kernel(blocks, *refs),
        [((rows + 16, channels), BF)],
        hbm(send_blocks[0, 0, 0].T),
        hbm(send_count[0, 0]),
        hbm(ref_feat[0, 0, 0]),
    )
    turn_shapes = [
        jax.ShapeDtypeStruct((channels, rows), BF),
        jax.ShapeDtypeStruct((rim, channels), BF),
        jax.ShapeDtypeStruct((offsets, 1, rows), jnp.int32),
        jax.ShapeDtypeStruct((offsets * channels, channels), BF),
    ]
    turn_inputs = [
        hbm(current),
        hbm(rim_rows[0, 0]),
        hbm(nbr.reshape(offsets, 1, rows)),
        hbm(conv_weight.reshape(offsets * channels, channels)),
    ]
    turned, picked, index, stack = pl.pallas_call(
        turn_kernel,
        grid=(1,),
        out_shape=turn_shapes,
        in_specs=[whole(*operand.shape) for operand in turn_inputs]
        + [pl.BlockSpec(memory_space=pl.ANY)],
        out_specs=[whole(*shape.shape) for shape in turn_shapes],
        compiler_params=params(),
    )(*turn_inputs, source)
    source = shifted(source, "ta", frames, 1)
    near_rim = swapped(picked, X, xcount, 0)
    far_rim = swapped(picked, X, xcount, 1)
    packed = simple(
        lambda *refs: pack_kernel(blocks, *refs),
        [((bricks, 32, channels), BF)],
        hbm(match_slot[0, 0]),
        source,
    )
    first = lax.all_to_all(packed, PLANE, split_axis=0, concat_axis=0, tiled=True)

    groups = offsets // GROUP
    index_spec = pl.BlockSpec((GROUP, 1, rows), lambda g: (g, 0, 0))
    weight_spec = pl.BlockSpec((GROUP * channels, channels), lambda g: (g, 0))

    part = GROUP * channels
    away_shape = pltpu.HBM((2 * part, rows), BF)
    kept_shape = jax.ShapeDtypeStruct((part, rows), BF)
    away_spec = pl.BlockSpec(memory_space=pl.ANY)
    away, kept, rims = pl.pallas_call(
        local_kernel,
        grid=(1,),
        out_shape=(away_shape, kept_shape, jax.ShapeDtypeStruct((3 * rim, channels), BF)),
        in_specs=[whole(offsets, 1, rows), whole(channels, rows)] + [whole(rim, channels)] * 3,
        out_specs=(away_spec, whole(part, rows), whole(3 * rim, channels)),
        scratch_shapes=[pltpu.VMEM((2, part, rows), BF), pltpu.SemaphoreType.DMA((2,))],
        compiler_params=params(24),
        cost_estimate=cost(4 * offsets * rows * rows * channels, 6e6),
    )(index, turned, near_rim, picked, far_rim)
    near_rims = swapped(rims, "gy", ycount, 0)
    far_rims = swapped(rims, "gy", ycount, 1)

    chosen = simple(
        lambda *refs: select_kernel(blocks, *refs), [((bricks, 24, channels), BF)], first
    )
    second = lax.all_to_all(chosen, PLANE, split_axis=0, concat_axis=0, tiled=True)

    away, kept, conv = pl.pallas_call(
        halo_kernel,
        grid=(1,),
        out_shape=(away_shape, kept_shape, jax.ShapeDtypeStruct((channels, rows), F32)),
        in_specs=[
            whole(offsets, 1, rows),
            whole(3 * rim, channels),
            whole(3 * rim, channels),
            whole(3 * rim, channels),
            whole(offsets * channels, channels),
            whole(part, rows),
            away_spec,
        ],
        out_specs=(away_spec, whole(part, rows), whole(channels, rows)),
        scratch_shapes=[
            pltpu.VMEM((channels, halo), BF),
            pltpu.VMEM((3, part, rows), BF),
            pltpu.SemaphoreType.DMA((2,)),
            pltpu.SemaphoreType.DMA((2,)),
        ],
        compiler_params=params(28),
        cost_estimate=cost(4 * offsets * rows * (halo + channels) * channels, 12e6),
    )(index, rims, near_rims, far_rims, stack, kept, hbm(away))

    half = 16 * channels
    activ, grad_turned, mine, other = pl.pallas_call(
        point_kernel,
        grid=(1,),
        out_shape=(
            jax.ShapeDtypeStruct((rows, channels), BF),
            jax.ShapeDtypeStruct((channels, rows), BF),
            jax.ShapeDtypeStruct((half, channels), BF),
            jax.ShapeDtypeStruct((half, channels), BF),
        ),
        in_specs=[
            whole(channels, rows),
            whole(bricks, 24, channels),
            whole(1, rows),
            whole(channels, channels),
            whole(1, channels),
            whole(part, rows),
            away_spec,
        ],
        out_specs=(
            whole(rows, channels),
            whole(channels, rows),
            whole(half, channels),
            whole(half, channels),
        ),
        scratch_shapes=[
            pltpu.VMEM((rows, channels), BF),
            pltpu.VMEM((2, part, rows), BF),
            pltpu.SemaphoreType.DMA((2,)),
        ],
        compiler_params=params(24),
    )(
        conv,
        second,
        hbm(labels[0, 0]),
        hbm(ref_weight),
        hbm(cls_weight[None, :]),
        kept,
        hbm(away),
    )

    got = lax.ppermute(other, "gc", [(0, 1), (1, 0)])
    chips = frames * lax.axis_size("gz") * ycount
    share = half // chips
    summed = (mine.astype(F32) + got.astype(F32)).astype(BF).reshape(chips, share, channels)
    summed = lax.all_to_all(summed, REST, split_axis=0, concat_axis=0, tiled=True)

    third = (halo // 3, channels)
    own, near, mid, far = pl.pallas_call(
        lambda *refs: grad_kernel(768, *refs),
        grid=(groups,),
        out_shape=(
            jax.ShapeDtypeStruct((rows, channels), F32),
            jax.ShapeDtypeStruct(third, BF),
            jax.ShapeDtypeStruct(third, F32),
            jax.ShapeDtypeStruct(third, BF),
        ),
        in_specs=[index_spec, whole(channels, rows), weight_spec],
        out_specs=(whole(rows, channels), whole(*third), whole(*third), whole(*third)),
        scratch_shapes=[
            pltpu.VMEM((channels, rows + halo), F32),
            pltpu.VMEM((channels, GROUP * rows), BF),
        ],
        compiler_params=params(32),
        cost_estimate=cost(4 * offsets * rows * (rows + halo) * channels, 4e6),
    )(index, grad_turned, stack)
    total = simple(sum_kernel, [((chips, share, channels), BF)], summed, mid)
    total = lax.all_to_all(total, REST, split_axis=0, concat_axis=0, tiled=True)
    near = swapped(near, X, xcount, 0)
    far = swapped(far, X, xcount, 1)
    third = (rim, channels)
    near, mid, far = simple(
        column_kernel, [(third, BF), (third, F32), (third, BF)], mid, near, far
    )
    near = swapped(near, "gy", ycount, 0)
    far = swapped(far, "gy", ycount, 1)
    feature_grad = simple(
        join_kernel, [((rows, channels), BF)], own, mid, near, far, hbm(rim_rows[0, 0])
    )
    feature_grad, total = lax.optimization_barrier((feature_grad, total))
    total = total.reshape(half, channels)
    partner = lax.ppermute(total, "gc", [(0, 1), (1, 0)])
    weight_grad, ref_grad = simple(
        finish_kernel,
        [((offsets * channels, channels), F32), ((channels, channels), F32)],
        total,
        partner,
    )
    weight_grad = weight_grad.reshape(offsets, channels, channels)
    return (activ[None, None, None], feature_grad[None, None, None], weight_grad, ref_grad)


def solution(mesh):
    frames, xcount, ycount = (mesh.shape[name] for name in ("ta", "gx", "gy"))
    fine = Mesh(
        mesh.devices.reshape(frames, xcount // 2, 2, ycount), ("ta", "gz", "gc", "gy")
    )
    three = P("ta", X, "gy", None)
    four = P("ta", X, "gy", None, None)
    placed = (four, four, three, four, four, three, three, three, P(), P(), P())
    return jax.shard_map(
        per_device,
        mesh=fine,
        in_specs=placed,
        out_specs=(four, four, P(), P()),
        check_vma=False,
    )
```

```python
import jax
import jax.numpy as jnp
from jax import lax
from jax.experimental import pallas as pl
from jax.experimental.pallas import tpu as pltpu
from jax.sharding import Mesh
from jax.sharding import PartitionSpec as P

BF = jnp.bfloat16
F32 = jnp.float32
I16 = jnp.int16
BLOCK = 128
LANES = 128
CAP = 2
GROUP = 9
LOSS_SCALE = 16.0
NT = (((1,), (1,)), ((), ()))
TN = (((0,), (0,)), ((), ()))
X = ("gz", "gc")
PLANE = ("gz", "gc", "gy")
REST = ("ta", "gz", "gy")


def params(mebibytes=16):
    return pltpu.CompilerParams(vmem_limit_bytes=mebibytes * 1024 * 1024)


def cost(flops, moved):
    return pl.CostEstimate(flops=int(flops), bytes_accessed=int(moved), transcendentals=0)


def iota(shape, dim):
    return lax.broadcasted_iota(jnp.int32, shape, dim)


def dot(left, right):
    return jnp.dot(left, right, preferred_element_type=F32)


def hot_of(mask):
    return jnp.where(mask, jnp.ones((), BF), jnp.zeros((), BF))


def lane_hot(column, width):
    n = column.shape[0]
    lane = iota((n, LANES), 1).astype(I16)
    column = column.astype(I16)
    pieces = []
    for start in range(0, width, LANES):
        piece = hot_of(column - jnp.asarray(start, I16) == lane)
        pieces.append(piece[:, : min(LANES, width - start)])
    return jnp.concatenate(pieces, axis=1) if len(pieces) > 1 else pieces[0]


def sublane_hot(row, start, height, width):
    base = iota((height, width), 0).astype(I16)
    rows = jnp.broadcast_to(row - start, (16, width)).astype(I16)
    wide = jnp.broadcast_to(rows[None], (height // 16, 16, width)).reshape(height, width)
    return hot_of(wide == base)


def list_kernel(blocks, lists_ref, counts_ref, source_ref, out_ref):
    dests = lists_ref.shape[1]
    lane = iota((dests, LANES), 1)
    dest = iota((dests, LANES), 0)
    row = jnp.zeros((1, LANES), F32)
    for c in range(CAP):
        listed = jnp.where(counts_ref[...] > c, lists_ref[c : c + 1, :], blocks).astype(F32)
        entry = jnp.broadcast_to(listed, (LANES, dests)).T
        row += jnp.sum(jnp.where(lane == dest * CAP + c, entry, 0.0), axis=0, keepdims=True)
    height = source_ref.shape[0]
    out_ref[0:height, :] = source_ref[...]
    first = iota((16, LANES), 0) == 0
    out_ref[height : height + 16, :] = jnp.where(first, row, 0.0).astype(BF)


def turn_kernel(
    current_ref, rim_ref, idx_ref, w_ref, after_ref, turned_ref, picked_ref, idx_out, w_out
):
    idx_out[...] = idx_ref[...]
    w_out[...] = w_ref[...]
    count = rim_ref.shape[1]
    turned = current_ref[...].T
    turned_ref[...] = turned
    hot = hot_of(iota((current_ref.shape[0], count), 0) == rim_ref[...])
    picked_ref[...] = dot(turned, hot).T.astype(BF)


def pack_kernel(blocks, match_ref, shift_ref, out_ref):
    bricks = out_ref.shape[0]
    step = BLOCK // bricks
    n = bricks * 32
    rows = iota((n, LANES), 0)
    i, j = rows // 32, rows % 32
    used = blocks * step
    target = jnp.where(
        j < used,
        (j // step) * BLOCK + i * step + j % step,
        jnp.where(j == used, blocks * BLOCK, -1),
    )
    hot = lane_hot(target, shift_ref.shape[0])
    out = dot(hot, shift_ref[...])
    wanted = jnp.broadcast_to(match_ref[...], (8, blocks)).astype(F32).astype(BF)
    slots = dot(wanted, hot_of(iota((blocks, LANES), 0) == iota((blocks, LANES), 1)))[0:1]
    out = jnp.where(j == used + 1, slots, out).astype(BF)
    out_ref[...] = out.reshape(bricks, 32, LANES)


def select_kernel(blocks, recv_ref, out_ref):
    bricks = out_ref.shape[0]
    step = BLOCK // bricks
    used = blocks * step
    room = out_ref.shape[1]
    n = bricks * room
    tail = recv_ref[:, 16:32, :].astype(F32)
    which = iota(tail.shape, 1)
    coded = jnp.sum(jnp.where(which == used - 16, tail, 0.0), axis=1).astype(BF)
    slots = jnp.sum(jnp.where(which == used - 15, tail, 0.0), axis=1).astype(BF)
    rows = iota((n, LANES), 0)
    lane = iota((n, LANES), 1)
    d, j = rows // room, rows % room
    own = hot_of(d == lane)[:, :bricks]
    listed = dot(own, slots)
    slot = jnp.sum(jnp.where(lane == j // step, listed, 0.0), axis=1, keepdims=True)
    slot = jnp.broadcast_to(slot, (n, LANES)).astype(jnp.int32)
    entry = hot_of(lane == d * CAP + slot % CAP)
    codes = lax.dot_general(entry, coded, NT, preferred_element_type=F32)
    source = slot // CAP
    code = jnp.sum(
        jnp.where(lane[:, :bricks] == source[:, :bricks], codes, 0.0), axis=1, keepdims=True
    )
    code = jnp.broadcast_to(code, (n, LANES)).astype(jnp.int32)
    live = (slot < bricks * CAP) & (code < blocks) & (j < used)
    index = jnp.where(live, source * 32 + code * step + j % step, -1)
    data = recv_ref[...].reshape(bricks * 32, LANES)
    out_ref[...] = dot(lane_hot(index, bricks * 32), data).astype(BF).reshape(out_ref.shape)


def local_kernel(
    idx_ref, turned_ref, near_ref, rim_ref, far_ref, away_ref, kept_ref, rims_ref, held_ref, sems
):
    count = rim_ref.shape[0]
    for n, part_ref in enumerate((near_ref, rim_ref, far_ref)):
        rims_ref[n * count : (n + 1) * count, :] = part_ref[...]
    height, width = turned_ref.shape[1], kept_ref.shape[1]
    part = kept_ref.shape[0]
    copies = []
    for g in range(idx_ref.shape[0] // GROUP):
        target = held_ref.at[g] if g < held_ref.shape[0] else kept_ref
        for o in range(GROUP):
            hot = sublane_hot(idx_ref[g * GROUP + o], 0, height, width)
            target[o * LANES : (o + 1) * LANES, :] = dot(turned_ref[...], hot).astype(BF)
        if g < held_ref.shape[0]:
            copy = pltpu.make_async_copy(
                held_ref.at[g], away_ref.at[pl.ds(g * part, part)], sems.at[g]
            )
            copy.start()
            copies.append(copy)
    for copy in copies:
        copy.wait()


def halo_kernel(
    idx_ref, rims_ref, near_ref, far_ref, w_ref, kept_in_ref, away_in_ref,
    away_ref, kept_ref, conv_ref, turned_ref, held_ref, in_sems, out_sems,
):
    width, part = kept_ref.shape[1], kept_ref.shape[0]
    rim = rims_ref.shape[0] // 3
    fetches = [
        pltpu.make_async_copy(
            away_in_ref.at[pl.ds(g * part, part)], held_ref.at[g], in_sems.at[g]
        )
        for g in range(2)
    ]
    for fetch in fetches:
        fetch.start()
    pieces = []
    even_x = lax.axis_index(X) % 2 == 0
    even_y = lax.axis_index("gy") % 2 == 0
    for i in range(3):
        third = 1 if i == 1 else jnp.where(even_x == (i == 2), 0, 2)
        rows = pl.ds(pl.multiple_of(third * rim, 16), rim)
        near, far = near_ref[rows, :].astype(F32), far_ref[rows, :].astype(F32)
        pieces.append(jnp.where(even_y, far, near))
        pieces.append(rims_ref[rows, :].astype(F32))
        pieces.append(jnp.where(even_y, near, far))
    turned_ref[...] = jnp.concatenate(pieces, axis=0).astype(BF).T
    stores = []
    for n, g in enumerate((2, 0, 1)):
        if n > 0:
            fetches[g].wait()
        source = kept_in_ref if n == 0 else held_ref.at[g]
        target = kept_ref if n == 2 else held_ref.at[2 - 2 * n]
        for o in range(GROUP):
            hot = sublane_hot(idx_ref[g * GROUP + o], width, 9 * rim, width)
            value = dot(turned_ref[...], hot).astype(BF)
            span = slice(o * LANES, (o + 1) * LANES)
            target[span, :] = source[span, :] + value
        weight = w_ref[g * part : (g + 1) * part, :]
        term = lax.dot_general(weight, target[...], TN, preferred_element_type=F32)
        conv_ref[...] = term if n == 0 else conv_ref[...] + term
        if n < 2:
            store = pltpu.make_async_copy(
                target, away_ref.at[pl.ds(n * part, part)], out_sems.at[n]
            )
            store.start()
            stores.append(store)
    for store in stores:
        store.wait()


def point_kernel(
    conv_ref, recv_ref, label_ref, ref_w_ref, cls_ref, kept_ref, away_ref,
    activ_ref, turned_ref, mine_ref, other_ref, grad_ref, held_ref, sems,
):
    groups, part = held_ref.shape[0] + 1, held_ref.shape[1]
    copies = [
        pltpu.make_async_copy(
            away_ref.at[pl.ds(n * part, part)], held_ref.at[n], sems.at[n]
        )
        for n in range(groups - 1)
    ]
    for copy in copies:
        copy.start()
    width = conv_ref.shape[1]
    core = lax.axis_index("gc")
    half = mine_ref.shape[0]

    def put(first, value):
        into_mine = (first // half) == core
        at = slice(first % half, first % half + value.shape[0])

        @pl.when(into_mine)
        def _():
            mine_ref[at, :] = value

        @pl.when(jnp.logical_not(into_mine))
        def _():
            other_ref[at, :] = value

    bricks, room = recv_ref.shape[0], recv_ref.shape[1]
    step = BLOCK // bricks
    v = iota((1, width), 1)
    place = ((v % BLOCK) // step) * room + (v // BLOCK) * step + v % step
    hot = sublane_hot(place, 0, bricks * room, width)
    matched = dot(recv_ref[...].reshape(bricks * room, LANES).T, hot).astype(BF)
    preact = conv_ref[...] + lax.dot_general(
        ref_w_ref[...], matched, TN, preferred_element_type=F32
    )
    cls = jnp.broadcast_to(cls_ref[...].astype(F32), (8, LANES)).T[:, 0:1]
    sig = jax.nn.sigmoid(preact)
    activ = (preact * sig).astype(BF)
    wide = activ.astype(F32)
    logits = jnp.sum(wide * cls, axis=0, keepdims=True)
    resid = jax.nn.sigmoid(logits) - label_ref[...].astype(F32)
    grad = LOSS_SCALE * resid * cls * sig * (1.0 + preact * (1.0 - sig))
    activ_ref[...] = activ.T
    turned_ref[...] = grad.astype(BF)
    grad_ref[...] = grad.astype(BF).T
    put(groups * part, dot(matched, grad_ref[...]).astype(BF))
    used = groups * part + LANES
    put(used, jnp.zeros((2 * half - used, LANES), BF))
    for n, g in enumerate((1, 2, 0)):
        if n > 0:
            copies[n - 1].wait()
        held = kept_ref[...] if n == 0 else held_ref[n - 1]
        terms = dot(held, grad_ref[...]).astype(BF)
        for o in range(part // LANES):
            put(g * part + o * LANES, terms[o * LANES : (o + 1) * LANES])


def add_rows(start, piece, idx_ref, grad_ref, w_ref, acc_ref, spread_ref):
    width, height = grad_ref.shape[1], acc_ref.shape[1]
    parts = dot(w_ref[...], grad_ref[...]).astype(BF)
    for o in range(GROUP):
        spread_ref[:, o * width : (o + 1) * width] = parts[o * LANES : (o + 1) * LANES]
    rows = jnp.concatenate(
        [idx_ref[o] for o in range(GROUP)] + [jnp.zeros((16 - GROUP, width), jnp.int32)], axis=0
    )
    columns = (rows - start).T
    starts = list(range(0, height - piece + 1, piece))
    for first, end in zip(starts, starts[1:] + [height]):
        size = end - first
        hot = jnp.concatenate(
            [
                lane_hot(jnp.broadcast_to(columns[:, o : o + 1] - first, (width, LANES)), size)
                for o in range(GROUP)
            ],
            axis=0,
        )
        acc_ref[:, first : first + size] += dot(spread_ref[...], hot)


def grad_kernel(
    piece, idx_ref, grad_ref, w_ref, own_ref, near_ref, mid_ref, far_ref, acc_ref, spread_ref
):
    @pl.when(pl.program_id(0) == 0)
    def _():
        acc_ref[...] = jnp.zeros_like(acc_ref)

    add_rows(0, piece, idx_ref, grad_ref, w_ref, acc_ref, spread_ref)

    @pl.when(pl.program_id(0) == pl.num_programs(0) - 1)
    def _():
        own, third = own_ref.shape[0], near_ref.shape[0]
        total = acc_ref[...].T
        even = lax.axis_index(X) % 2 == 0
        low = total[own : own + third].astype(BF)
        high = total[own + 2 * third : own + 3 * third].astype(BF)
        own_ref[...] = total[0:own]
        near_ref[...] = jnp.where(even, high, low)
        mid_ref[...] = total[own + third : own + 2 * third]
        far_ref[...] = jnp.where(even, low, high)


def join_kernel(own_ref, mid_ref, low_ref, high_ref, rim_ref, out_ref):
    total = mid_ref[...] + low_ref[...].astype(F32) + high_ref[...].astype(F32)
    upper = total.astype(BF)
    lower = (total - upper.astype(F32)).astype(BF)
    height, count = out_ref.shape[0], total.shape[0]
    hot = hot_of(iota((height, count), 0) == rim_ref[...])
    out_ref[...] = (own_ref[...] + dot(hot, upper) + dot(hot, lower)).astype(BF)


def column_kernel(mid_ref, near_in_ref, far_in_ref, near_ref, mine_ref, far_ref):
    total = mid_ref[...] + near_in_ref[...].astype(F32) + far_in_ref[...].astype(F32)
    third = total.shape[0] // 3
    even = lax.axis_index("gy") % 2 == 0
    low = total[0:third].astype(BF)
    high = total[2 * third : 3 * third].astype(BF)
    near_ref[...] = jnp.where(even, high, low)
    mine_ref[...] = total[third : 2 * third]
    far_ref[...] = jnp.where(even, low, high)


def sum_kernel(parts_ref, after_ref, out_ref):
    total = jnp.sum(parts_ref[...].astype(F32), axis=0).astype(BF)
    out_ref[...] = jnp.broadcast_to(total[None], out_ref.shape)


def finish_kernel(mine_ref, other_ref, weight_ref, ref_ref):
    core = lax.axis_index("gc")
    half = mine_ref.shape[0]
    rest = weight_ref.shape[0] - half
    tail = ref_ref.shape[0]

    def write(low_ref, high_ref):
        weight_ref[0:half, :] = low_ref[...].astype(F32)
        weight_ref[half : half + rest, :] = high_ref[0:rest, :].astype(F32)
        ref_ref[...] = high_ref[rest : rest + tail, :].astype(F32)

    @pl.when(core == 0)
    def _():
        write(mine_ref, other_ref)

    @pl.when(core != 0)
    def _():
        write(other_ref, mine_ref)


def shifted(block, axis, count, distance):
    route = [(i - distance, i) for i in range(count) if 0 <= i - distance < count]
    return lax.ppermute(block, axis, route)


def swapped(block, axis, count, start):
    route = []
    for i in range(start, count - 1, 2):
        route += [(i, i + 1), (i + 1, i)]
    return lax.ppermute(block, axis, route)


def per_device(
    feat,
    ref_feat,
    rim_rows,
    nbr,
    send_blocks,
    send_count,
    match_slot,
    labels,
    conv_weight,
    ref_weight,
    cls_weight,
):
    current = feat[0, 0, 0]
    rows, channels = current.shape
    blocks = rows // BLOCK
    rim = rim_rows.shape[3]
    offsets = nbr.shape[3]
    frames, ycount = lax.axis_size("ta"), lax.axis_size("gy")
    xcount = lax.axis_size(X)
    bricks = xcount * ycount
    halo = 9 * rim

    def whole(*shape):
        return pl.BlockSpec(shape, lambda g: (0,) * len(shape))

    def simple(kernel, shapes, *operands):
        shapes = [jax.ShapeDtypeStruct(*shape) for shape in shapes]
        specs = [whole(*shape.shape) for shape in shapes]
        one = len(shapes) == 1
        return pl.pallas_call(
            kernel,
            grid=(1,),
            out_shape=shapes[0] if one else shapes,
            in_specs=[whole(*operand.shape) for operand in operands],
            out_specs=specs[0] if one else specs,
            compiler_params=params(),
        )(*operands)

    def hbm(operand):
        return pltpu.with_memory_space_constraint(operand, pltpu.HBM)

    source = simple(
        lambda *refs: list_kernel(blocks, *refs),
        [((rows + 16, channels), BF)],
        hbm(send_blocks[0, 0, 0].T),
        hbm(send_count[0, 0]),
        hbm(ref_feat[0, 0, 0]),
    )
    turn_shapes = [
        jax.ShapeDtypeStruct((channels, rows), BF),
        jax.ShapeDtypeStruct((rim, channels), BF),
        jax.ShapeDtypeStruct((offsets, 1, rows), jnp.int32),
        jax.ShapeDtypeStruct((offsets * channels, channels), BF),
    ]
    turn_inputs = [
        hbm(current),
        hbm(rim_rows[0, 0]),
        hbm(nbr.reshape(offsets, 1, rows)),
        hbm(conv_weight.reshape(offsets * channels, channels)),
    ]
    turned, picked, index, stack = pl.pallas_call(
        turn_kernel,
        grid=(1,),
        out_shape=turn_shapes,
        in_specs=[whole(*operand.shape) for operand in turn_inputs]
        + [pl.BlockSpec(memory_space=pl.ANY)],
        out_specs=[whole(*shape.shape) for shape in turn_shapes],
        compiler_params=params(),
    )(*turn_inputs, source)
    source = shifted(source, "ta", frames, 1)
    near_rim = swapped(picked, X, xcount, 0)
    far_rim = swapped(picked, X, xcount, 1)
    packed = simple(
        lambda *refs: pack_kernel(blocks, *refs),
        [((bricks, 32, channels), BF)],
        hbm(match_slot[0, 0]),
        source,
    )
    first = lax.all_to_all(packed, PLANE, split_axis=0, concat_axis=0, tiled=True)

    groups = offsets // GROUP
    index_spec = pl.BlockSpec((GROUP, 1, rows), lambda g: (g, 0, 0))
    weight_spec = pl.BlockSpec((GROUP * channels, channels), lambda g: (g, 0))

    part = GROUP * channels
    away_shape = pltpu.HBM((2 * part, rows), BF)
    kept_shape = jax.ShapeDtypeStruct((part, rows), BF)
    away_spec = pl.BlockSpec(memory_space=pl.ANY)
    away, kept, rims = pl.pallas_call(
        local_kernel,
        grid=(1,),
        out_shape=(away_shape, kept_shape, jax.ShapeDtypeStruct((3 * rim, channels), BF)),
        in_specs=[whole(offsets, 1, rows), whole(channels, rows)] + [whole(rim, channels)] * 3,
        out_specs=(away_spec, whole(part, rows), whole(3 * rim, channels)),
        scratch_shapes=[pltpu.VMEM((2, part, rows), BF), pltpu.SemaphoreType.DMA((2,))],
        compiler_params=params(24),
        cost_estimate=cost(4 * offsets * rows * rows * channels, 6e6),
    )(index, turned, near_rim, picked, far_rim)
    near_rims = swapped(rims, "gy", ycount, 0)
    far_rims = swapped(rims, "gy", ycount, 1)

    chosen = simple(
        lambda *refs: select_kernel(blocks, *refs), [((bricks, 24, channels), BF)], first
    )
    second = lax.all_to_all(chosen, PLANE, split_axis=0, concat_axis=0, tiled=True)

    away, kept, conv = pl.pallas_call(
        halo_kernel,
        grid=(1,),
        out_shape=(away_shape, kept_shape, jax.ShapeDtypeStruct((channels, rows), F32)),
        in_specs=[
            whole(offsets, 1, rows),
            whole(3 * rim, channels),
            whole(3 * rim, channels),
            whole(3 * rim, channels),
            whole(offsets * channels, channels),
            whole(part, rows),
            away_spec,
        ],
        out_specs=(away_spec, whole(part, rows), whole(channels, rows)),
        scratch_shapes=[
            pltpu.VMEM((channels, halo), BF),
            pltpu.VMEM((3, part, rows), BF),
            pltpu.SemaphoreType.DMA((2,)),
            pltpu.SemaphoreType.DMA((2,)),
        ],
        compiler_params=params(28),
        cost_estimate=cost(4 * offsets * rows * (halo + channels) * channels, 12e6),
    )(index, rims, near_rims, far_rims, stack, kept, hbm(away))

    half = 16 * channels
    activ, grad_turned, mine, other = pl.pallas_call(
        point_kernel,
        grid=(1,),
        out_shape=(
            jax.ShapeDtypeStruct((rows, channels), BF),
            jax.ShapeDtypeStruct((channels, rows), BF),
            jax.ShapeDtypeStruct((half, channels), BF),
            jax.ShapeDtypeStruct((half, channels), BF),
        ),
        in_specs=[
            whole(channels, rows),
            whole(bricks, 24, channels),
            whole(1, rows),
            whole(channels, channels),
            whole(1, channels),
            whole(part, rows),
            away_spec,
        ],
        out_specs=(
            whole(rows, channels),
            whole(channels, rows),
            whole(half, channels),
            whole(half, channels),
        ),
        scratch_shapes=[
            pltpu.VMEM((rows, channels), BF),
            pltpu.VMEM((2, part, rows), BF),
            pltpu.SemaphoreType.DMA((2,)),
        ],
        compiler_params=params(24),
    )(
        conv,
        second,
        hbm(labels[0, 0]),
        hbm(ref_weight),
        hbm(cls_weight[None, :]),
        kept,
        hbm(away),
    )

    got = lax.ppermute(other, "gc", [(0, 1), (1, 0)])
    chips = frames * lax.axis_size("gz") * ycount
    share = half // chips
    summed = (mine.astype(F32) + got.astype(F32)).astype(BF).reshape(chips, share, channels)
    summed = lax.all_to_all(summed, REST, split_axis=0, concat_axis=0, tiled=True)

    third = (halo // 3, channels)
    own, near, mid, far = pl.pallas_call(
        lambda *refs: grad_kernel(384, *refs),
        grid=(groups,),
        out_shape=(
            jax.ShapeDtypeStruct((rows, channels), F32),
            jax.ShapeDtypeStruct(third, BF),
            jax.ShapeDtypeStruct(third, F32),
            jax.ShapeDtypeStruct(third, BF),
        ),
        in_specs=[index_spec, whole(channels, rows), weight_spec],
        out_specs=(whole(rows, channels), whole(*third), whole(*third), whole(*third)),
        scratch_shapes=[
            pltpu.VMEM((channels, rows + halo), F32),
            pltpu.VMEM((channels, GROUP * rows), BF),
        ],
        compiler_params=params(32),
        cost_estimate=cost(4 * offsets * rows * (rows + halo) * channels, 4e6),
    )(index, grad_turned, stack)
    total = simple(sum_kernel, [((chips, share, channels), BF)], summed, mid)
    total = lax.all_to_all(total, REST, split_axis=0, concat_axis=0, tiled=True)
    near = swapped(near, X, xcount, 0)
    far = swapped(far, X, xcount, 1)
    third = (rim, channels)
    near, mid, far = simple(
        column_kernel, [(third, BF), (third, F32), (third, BF)], mid, near, far
    )
    near = swapped(near, "gy", ycount, 0)
    far = swapped(far, "gy", ycount, 1)
    feature_grad = simple(
        join_kernel, [((rows, channels), BF)], own, mid, near, far, hbm(rim_rows[0, 0])
    )
    feature_grad, total = lax.optimization_barrier((feature_grad, total))
    total = total.reshape(half, channels)
    partner = lax.ppermute(total, "gc", [(0, 1), (1, 0)])
    weight_grad, ref_grad = simple(
        finish_kernel,
        [((offsets * channels, channels), F32), ((channels, channels), F32)],
        total,
        partner,
    )
    weight_grad = weight_grad.reshape(offsets, channels, channels)
    return (activ[None, None, None], feature_grad[None, None, None], weight_grad, ref_grad)


def solution(mesh):
    frames, xcount, ycount = (mesh.shape[name] for name in ("ta", "gx", "gy"))
    fine = Mesh(
        mesh.devices.reshape(frames, xcount // 2, 2, ycount), ("ta", "gz", "gc", "gy")
    )
    three = P("ta", X, "gy", None)
    four = P("ta", X, "gy", None, None)
    placed = (four, four, three, four, four, three, three, three, P(), P(), P())
    return jax.shard_map(
        per_device,
        mesh=fine,
        in_specs=placed,
        out_specs=(four, four, P(), P()),
        check_vma=False,
    )
```
